512 devices in a mesh: row: 16 (over z, core), col: 32 (over y, x).
Axes of the slice: x: 4, y: 8, z: 8, core: 2. Of those that a mesh axis runs over, the one named last changes fastest.
Arguments:
- row_bases: float32 [16, 512, 4096], P('row', 'col'), may hold values from -4 to 4, as said below
- col_bases: float32 [32, 256, 4096], P('col', 'row'), may hold values from -4 to 4, as said below
- row_transfer: float32 [16, 1024, 4096], P('row', 'col'), may hold values from -1 to 1, as said below
- col_transfer: float32 [32, 512, 4096], P('col', 'row'), may hold values from -1 to 1, as said below
- row_order: int32 [16, 32, 16], P('row', 'col'), may hold values from 0 to 15, each once within a row
- col_order: int32 [32, 16, 16], P('col', 'row'), may hold values from 0 to 15, each once within a row
- leaf_pattern: int32 [16, 64, 64], P('row', 'col'), may hold values from 0 to 15
- leaf_blocks: bfloat16 [16, 2048, 4096], P('row', 'col'), may hold values from -6 to 6
- root_rows: int32 [16, 32, 32], P('row', 'col'), may hold values from 0 to 31
- root_cols: int32 [16, 32, 32], P('row', 'col'), may hold values from 0 to 15
- root_blocks: bfloat16 [16, 1024, 4096], P('row', 'col'), may hold values from -6 to 6
Outputs:
- leaf_coupled: float32 [16, 2048, 4096], P('row', 'col')
- root_coupled: float32 [16, 1024, 4096], P('row', 'col')
- row_upper_r: float32 [16, 32, 4096], P('row', 'col')
- col_upper_r: float32 [32, 16, 4096], P('col', 'row')
The draws below stay inside these ranges and needn't reach their ends.
Inputs may be any that keep to these rules, and one draw needn't show every extreme that they name: `row_bases`: every leaf basis has full column rank and every Gram matrix of both trees is well conditioned. `col_bases`: every leaf basis has full column rank and every Gram matrix of both trees is well conditioned. `row_transfer`: every transfer matrix is invertible. `col_transfer`: every transfer matrix is invertible.
All inputs are finite; a program needn't handle non-finite values.
Results may differ from the reference program's by a relative error of at most 0.0003.
Values sent between devices are 32-bit elements; how exact they have to be, the bound alone decides.
A program may use at most 64 MiB of HBM per device.

```python
import math
import jax
import jax.numpy as jnp
from jax import lax

LEAF = 64
RANK = 64
LEAF_DEV = 16
LEAF_PAIRS = 64
ROOT_PAIRS = 32
N_ROW = 16
N_COL = 32


def basis_law(key, outer_count, inner_count):
    key_scale = jax.random.fold_in(key, 3)
    key_jitter = jax.random.fold_in(key, 5)
    scales = jnp.exp(jax.random.uniform(key_scale, (outer_count, inner_count, LEAF, 1), minval=math.log(0.5), maxval=math.log(2.0)))
    jitter = jax.random.truncated_normal(key_jitter, -4.0, 4.0, (outer_count, inner_count, LEAF, RANK))
    identity = jnp.eye(LEAF, RANK, dtype=jnp.float32)
    leaf_basis = scales * (identity + 0.25 * jitter / math.sqrt(RANK))
    return leaf_basis.reshape(outer_count, inner_count, LEAF * RANK)


def transfer_law(key, outer_count, inner_count):
    key_jitter = jax.random.fold_in(key, 7)
    jitter = jax.random.truncated_normal(key_jitter, -4.0, 4.0, (outer_count, inner_count, RANK, RANK))
    identity = jnp.eye(RANK, dtype=jnp.float32)
    matrices = 0.7 * (identity + 0.25 * jitter / math.sqrt(RANK))
    return matrices.reshape(outer_count, inner_count, RANK * RANK)


def draw_row_bases(key, part):
    return basis_law(jax.random.fold_in(key, 11), N_ROW, N_COL * LEAF_DEV)


def draw_col_bases(key, part):
    return basis_law(jax.random.fold_in(key, 13), N_COL, N_ROW * LEAF_DEV)


def draw_row_transfer(key, part):
    return transfer_law(jax.random.fold_in(key, 17), N_ROW, N_COL * 2 * LEAF_DEV)


def draw_col_transfer(key, part):
    return transfer_law(jax.random.fold_in(key, 19), N_COL, N_ROW * 2 * LEAF_DEV)


def with_ends(array, own_key, smallest, high):
    spot = [jax.random.randint(jax.random.fold_in(own_key, axis), (), 0, length) for axis, length in enumerate(array.shape)]
    main_axis = array.shape.index(max(array.shape))
    beside = spot[:main_axis] + [(spot[main_axis] + 1) % array.shape[main_axis]] + spot[main_axis + 1:]
    return array.at[tuple(spot)].set(smallest).at[tuple(beside)].set(high)


def steps_of(stream_key, dims, pieces, smallest, largest):
    def one(axis_at, parts):
        heights = jax.random.uniform(jax.random.fold_in(jax.random.fold_in(stream_key, 6), axis_at), (parts,), jnp.float32, smallest / len(pieces), largest / len(pieces))
        return jnp.repeat(jnp.exp(heights), dims[axis_at] // parts).reshape((-1,) + (1,) * (len(dims) - axis_at - 1))

    factor_of = one(*pieces[0])
    for cut in pieces[1:]:
        factor_of = factor_of * one(*cut)
    return factor_of


def normal_values(stream_key, shape, scale, limit, shards=(), kind=jnp.bfloat16):
    values = scale * jax.random.normal(stream_key, shape, jnp.float32)
    if shards:
        values = values * steps_of(stream_key, shape, shards, -0.22, 0.18)
    return jnp.clip(values, -limit, limit).astype(kind)


def setup_inputs(seed: int = 0) -> dict:
    streams_of = jax.random.split(jax.random.key(seed), 12)
    return {
        "row_bases": draw_row_bases(jax.random.fold_in(streams_of[11], 71), 0),
        "col_bases": draw_col_bases(jax.random.fold_in(streams_of[11], 71), 0),
        "row_transfer": draw_row_transfer(jax.random.fold_in(streams_of[11], 71), 0),
        "col_transfer": draw_col_transfer(jax.random.fold_in(streams_of[11], 71), 0),
        "row_order": jax.vmap(lambda own: jax.random.permutation(own, LEAF_DEV))(jax.random.split(streams_of[4], N_ROW * N_COL)).reshape((N_ROW, N_COL, LEAF_DEV)).astype(jnp.int32),
        "col_order": jax.vmap(lambda own: jax.random.permutation(own, LEAF_DEV))(jax.random.split(streams_of[5], N_COL * N_ROW)).reshape((N_COL, N_ROW, LEAF_DEV)).astype(jnp.int32),
        "leaf_pattern": with_ends(jax.random.randint(streams_of[6], (N_ROW, 2 * N_COL, LEAF_PAIRS), 0, LEAF_DEV), jax.random.fold_in(streams_of[6], 1), 0, LEAF_DEV - 1).astype(jnp.int32),
        "leaf_blocks": normal_values(streams_of[7], (N_ROW, N_COL * LEAF_PAIRS, RANK * RANK), 1.0, 6.0, ((0, 16), (1, 32))),
        "root_rows": with_ends(jax.random.randint(streams_of[8], (N_ROW, N_COL, ROOT_PAIRS), 0, N_COL), jax.random.fold_in(streams_of[8], 1), 0, N_COL - 1).astype(jnp.int32),
        "root_cols": with_ends(jax.random.randint(streams_of[9], (N_ROW, N_COL, ROOT_PAIRS), 0, N_ROW), jax.random.fold_in(streams_of[9], 1), 0, N_ROW - 1).astype(jnp.int32),
        "root_blocks": normal_values(streams_of[10], (N_ROW, N_COL * ROOT_PAIRS, RANK * RANK), 1.0, 6.0, ((0, 16), (1, 32))),
    }


def matmul_high(first_matrix, second_matrix):
    return jnp.matmul(first_matrix, second_matrix, precision=lax.Precision.HIGHEST)

def flipped(matrix):
    return jnp.swapaxes(matrix, -1, -2)

def sandwich(gram, transfer):
    return matmul_high(flipped(transfer), matmul_high(gram, transfer))

def upper_factor(gram):
    return flipped(jnp.linalg.cholesky(gram))

def tree_pass(bases, transfer, order):
    block_count = bases.shape[0]
    leaf_basis = bases.reshape(block_count, LEAF_DEV, LEAF, RANK)
    leaf_gram = jnp.einsum('bpla,bplc->bpac', leaf_basis, leaf_basis, precision=lax.Precision.HIGHEST)
    matrices = transfer.reshape(block_count, 2 * LEAF_DEV, RANK, RANK)
    block_index = jnp.arange(block_count, dtype=jnp.int32)[:, None]
    node_gram = leaf_gram[block_index, order]
    node_up = matrices[block_index, order]
    node_count = LEAF_DEV
    offset = LEAF_DEV
    while node_count > 1:
        contribution = sandwich(node_gram, node_up)
        node_gram = contribution[:, 0::2] + contribution[:, 1::2]
        node_count = node_count // 2
        node_up = matrices[:, offset:offset + node_count]
        offset = offset + node_count
    root_gram = node_gram[:, 0]
    inner_up = matrices[:, 2 * LEAF_DEV - 1]
    highest = root_gram
    node_gram = root_gram
    node_up = node_up[:, 0]
    stride = 1
    while stride < block_count:
        contribution = sandwich(node_gram, node_up)
        node_gram = contribution[0::2] + contribution[1::2]
        node_up = inner_up[stride::2 * stride]
        highest = highest.at[stride::2 * stride].set(node_gram)
        stride = stride * 2
    highest = highest.at[0].set(node_gram[0])
    return (upper_factor(leaf_gram), upper_factor(root_gram), upper_factor(highest))

def reference(row_bases, col_bases, row_transfer, col_transfer, row_order, col_order, leaf_pattern, leaf_blocks, root_rows, root_cols, root_blocks):
    total = N_ROW * N_COL
    row_leaf, row_root, row_high = tree_pass(row_bases.reshape(total, LEAF_DEV, LEAF * RANK), row_transfer.reshape(total, 2 * LEAF_DEV, RANK * RANK), row_order.reshape(total, LEAF_DEV))
    col_leaf, col_root, col_high = tree_pass(col_bases.reshape(total, LEAF_DEV, LEAF * RANK), col_transfer.reshape(total, 2 * LEAF_DEV, RANK * RANK), col_order.reshape(total, LEAF_DEV))
    row_leaf = row_leaf.reshape(N_ROW, N_COL, LEAF_DEV, RANK, RANK)
    col_leaf = jnp.swapaxes(col_leaf.reshape(N_COL, N_ROW, LEAF_DEV, RANK, RANK), 0, 1)
    pattern = leaf_pattern.reshape(N_ROW, N_COL, 2, LEAF_PAIRS)
    leaf_squares = leaf_blocks.astype(jnp.float32).reshape(N_ROW, N_COL, LEAF_PAIRS, RANK, RANK)
    column_index = jnp.arange(N_COL, dtype=jnp.int32)[:, None]

    def leaf_row(operands):
        row_factors, col_factors, pattern_row, squares = operands
        left_factor = row_factors[column_index, pattern_row[:, 0]]
        right_factor = col_factors[column_index, pattern_row[:, 1]]
        return matmul_high(matmul_high(left_factor, squares), flipped(right_factor))
    leaf_coupled = lax.map(leaf_row, (row_leaf, col_leaf, pattern, leaf_squares)).reshape(N_ROW, N_COL * LEAF_PAIRS, RANK * RANK)
    row_root = row_root.reshape(N_ROW, N_COL, RANK, RANK)
    col_root = col_root.reshape(N_COL, N_ROW, RANK, RANK)
    root_squares = root_blocks.astype(jnp.float32).reshape(N_ROW, N_COL, ROOT_PAIRS, RANK, RANK)

    def root_row(operands):
        row_factors, rows_here, cols_here, squares = operands
        left_factor = row_factors[rows_here]
        right_factor = col_root[column_index, cols_here]
        return matmul_high(matmul_high(left_factor, squares), flipped(right_factor))
    root_coupled = lax.map(root_row, (row_root, root_rows, root_cols, root_squares)).reshape(N_ROW, N_COL * ROOT_PAIRS, RANK * RANK)
    row_upper_r = row_high.reshape(N_ROW, N_COL, RANK * RANK)
    col_upper_r = col_high.reshape(N_COL, N_ROW, RANK * RANK)
    return (leaf_coupled, root_coupled, row_upper_r, col_upper_r)
```

```python
import functools

import jax
import jax.numpy as jnp
from jax import lax
from jax.experimental import pallas as pl
from jax.experimental.pallas import tpu as pltpu
from jax.sharding import PartitionSpec as P

RANK = 64
LEAF_DEV = 16
LEAF_PAIRS = 64
ROOT_PAIRS = 32
N_ROW = 16
N_COL = 32
N_X = 4
N_Y = 8
GROUP = 24
BATCH = 2 * GROUP
MESH = pl.DeviceIdType.MESH
F32 = jnp.float32
BF16 = jnp.bfloat16


def split(value):
    high = value.astype(BF16)
    return high, (value - high.astype(F32)).astype(BF16)


def contract(left, right, left_dim, right_dim):
    return lax.dot_general(
        left, right, (((left_dim,), (right_dim,)), ((), ())), preferred_element_type=F32
    )


def product_tn(left, right):
    left_high, left_low = split(left)
    right_high, right_low = split(right)
    return contract(
        jnp.concatenate([left_high, left_high, left_low], 0),
        jnp.concatenate([right_high, right_low, right_high], 0),
        0,
        0,
    )


def product_nn(left, right):
    left_high, left_low = split(left)
    right_high, right_low = split(right)
    both = contract(jnp.concatenate([left_high, left_low], 0), right_high, 1, 0)
    rows = left.shape[0]
    return both[:rows] + both[rows:] + contract(left_high, right_low, 1, 0)


def sandwich(gram, transfer):
    return product_tn(transfer, product_nn(gram, transfer))


def pack(square):
    return jnp.concatenate([square[:32, :], square[32:, :]], 1)


def unpack(packed):
    return jnp.concatenate([packed[:, :RANK], packed[:, RANK:]], 0)


def level_of(place, depth):
    level = jnp.int32(depth)
    for k in range(depth - 1, 0, -1):
        level = jnp.where(lax.rem(place, 1 << k) == 1 << (k - 1), jnp.int32(k), level)
    return level


def span_of(place, depth):
    span = jnp.int32(1 << depth)
    for k in range(depth - 1, 0, -1):
        span = jnp.where(lax.rem(place, 1 << k) == 1 << (k - 1), jnp.int32(1 << k), span)
    return span


def fixed_level(place, depth):
    return depth if place == 0 else (place & -place).bit_length()


class Stage:
    def __init__(self, depth, place, taking_part, peer, refs):
        self.depth, self.size, self.place = depth, 1 << depth, place
        self.taking_part, self.peer = taking_part, peer
        (self.inner, self.terms, self.slots, self.inner_sent, self.inner_got, self.sent, self.got) = refs
        self.level = level_of(place, depth)
        self.span = span_of(place, depth)

    def inner_copy(self, target, level):
        return pltpu.make_async_remote_copy(
            self.own_inner,
            self.inner.at[level - 1],
            self.inner_sent.at[target],
            self.inner_got.at[level - 1],
            device_id=self.peer(target),
            device_id_type=MESH,
        )

    def each_inner_target(self, act):
        for target in range(self.size):
            same = lax.div(self.place, self.span) == lax.div(jnp.int32(target), self.span)
            wanted = (self.place != 0) & (self.place != target) & same
            if target != 0:
                wanted = wanted & (self.span < self.size)
            pl.when(self.taking_part & wanted)(functools.partial(act, target))

    def send_inner(self, own_inner):
        self.own_inner = own_inner
        self.each_inner_target(lambda target: self.inner_copy(target, self.level).start())

    def receive_inner(self):
        for level in range(1, self.depth + 1):
            half = 1 << (level - 1)
            if level < self.depth:
                mine = lax.rem(self.place, 2 * half) == half
                away = jnp.logical_not(mine)

                @pl.when(self.taking_part & mine)
                def _(level=level):
                    self.inner[level - 1] = self.own_inner[...]
            else:
                away = self.place == 0

            @pl.when(self.taking_part & away)
            def _(level=level):
                self.inner_copy(0, level).wait_recv()

    def make_terms(self, gram, transfer):
        path = transfer
        for level in range(1, self.depth + 1):
            self.terms[level - 1] = pack(sandwich(gram, path))
            if level < self.depth:
                path = product_nn(path, unpack(self.inner[level - 1]))

    def term_copy(self, target, sender):
        return pltpu.make_async_remote_copy(
            self.terms.at[fixed_level(target, self.depth) - 1],
            self.slots.at[sender],
            self.sent.at[target],
            self.got.at[sender],
            device_id=self.peer(target),
            device_id_type=MESH,
        )

    def each_target(self, act):
        for target in range(self.size):
            span = 1 << fixed_level(target, self.depth)
            wanted = (self.place != target) & (lax.div(self.place, span) == target // span)
            pl.when(self.taking_part & wanted)(functools.partial(act, target))

    def send_terms(self):
        self.each_target(lambda target: self.term_copy(target, self.place).start())

    def receive_terms(self, total_ref):
        @pl.when(self.taking_part)
        def _():
            total_ref[...] = self.terms[self.level - 1]

        for sender in range(self.size):
            same = lax.div(self.place, self.span) == lax.div(jnp.int32(sender), self.span)

            @pl.when(self.taking_part & (self.place != sender) & same)
            def _(sender=sender):
                self.term_copy(0, sender).wait_recv()
                total_ref[...] += self.slots[sender]

    def finish(self):
        self.each_inner_target(lambda target: self.inner_copy(target, self.level).wait_send())
        self.each_target(lambda target: self.term_copy(target, self.place).wait_send())


def to_lanes(gram_ref, batch_ref, count):
    flat = gram_ref.reshape(BATCH * RANK, 128)

    def step(j, carry):
        rows = flat[pl.ds(j, count, stride=RANK), :]
        batch_ref[j, :, :count] = rows.T[:RANK, :]
        return carry

    lax.fori_loop(0, RANK, step, 0, unroll=8)


def factor(batch_ref):
    for block in range(8):
        first = 8 * block
        columns = [batch_ref[first + c, first:, :] for c in range(8)]
        for c in range(8):
            pivot = columns[c][c : c + 1, :]
            column = columns[c] * lax.rsqrt(pivot)
            columns[c] = column
            batch_ref[first + c, first:, :] = column
            for later in range(c + 1, 8):
                columns[later] = columns[later] - column * column[later : later + 1, :]
        for other in range(block + 1, 8):

            def update(step, carry, first=first, other=other):
                j = 8 * other + step
                total = batch_ref[j, 8 * other :, :]
                for c in range(8):
                    total = total - batch_ref[first + c, 8 * other :, :] * batch_ref[first + c, pl.ds(j, 1), :]
                batch_ref[j, 8 * other :, :] = total
                return carry

            lax.fori_loop(0, 8, update, 0, unroll=4)


def from_lanes(batch_ref, factor_ref, counts):
    lane = lax.broadcasted_iota(jnp.int32, (1, 128), 1)
    column = jnp.where(lane < 32, 2 * lane, jnp.where(lane < 64, 2 * lane - 63, lane - 64))

    def step(j, carry):
        plane = batch_ref.at[j]
        values = jnp.concatenate(
            [plane[pl.ds(0, 32, stride=2), :], plane[pl.ds(1, 32, stride=2), :], plane[...]], 0
        ).T
        values = jnp.where(column >= j, values[: sum(counts)], 0.0)
        moved = lax.div(j, 2) + 32 * lax.rem(j, 2)
        factor_ref[pl.ds(moved, counts[0], stride=RANK), :] = values[: counts[0]]
        if len(counts) > 1:
            factor_ref[pl.ds(counts[0] * RANK + j, counts[1], stride=RANK), :] = values[counts[0] :]
        return carry

    lax.fori_loop(0, RANK, step, 0, unroll=4)


def couple(count, blocks_ref, stage_ref, left_ref, right_ref, left_pick, right_pick, out_ref):
    def step(group, carry):
        base = pl.multiple_of(group * 256, 256)
        stage_ref[...] = blocks_ref[pl.ds(base, 256), :].astype(F32)
        for pair in range(8):
            packed = stage_ref[pl.ds(pair, 32, stride=8), :].astype(BF16)
            square = unpack(packed)
            left = left_ref[left_pick(group * 8 + pair)]
            right = right_ref[right_pick(group * 8 + pair)]
            both = contract(left, square, 1, 0)
            high, low = split(both[:RANK] + both[RANK:])
            out = contract(jnp.concatenate([high, low], 0), right[:RANK], 1, 1)
            out = out[:RANK] + out[RANK:] + contract(high, right[RANK:], 1, 1)
            out_ref[pl.ds(base + pair, 32, stride=8), :] = pack(out)
        return carry

    lax.fori_loop(0, count // 8, step, 0)


def table_entry(value):
    return jnp.concatenate(split(value), 0)


STAGES = ((2, 3, 4), (4, 2, 3))


def kernel(
    row_order,
    col_order,
    leaf_pattern,
    root_rows,
    root_cols,
    row_bases_hbm,
    col_bases_hbm,
    row_transfer_hbm,
    col_transfer_hbm,
    leaf_blocks_hbm,
    root_blocks_hbm,
    leaf_out,
    root_out,
    row_out,
    col_out,
    bases,
    transfers,
    leaf_blocks,
    root_blocks,
    loads,
    natural,
    grams,
    nodes,
    batch,
    factors,
    leaf_left,
    leaf_right,
    root_left,
    root_right,
    block_stage,
    inner_own,
    highest,
    row_own,
    col_own,
    row_table,
    col_table,
    row_sent,
    row_got,
    col_sent,
    col_got,
    *stage_refs,
):
    place_row = lax.axis_index("row")
    place_col = lax.axis_index("col")
    copies = [
        pltpu.make_async_copy(source, target, loads.at[n])
        for n, (source, target) in enumerate(
            [
                (row_bases_hbm, bases.at[0]),
                (col_bases_hbm, bases.at[1]),
                (row_transfer_hbm, transfers.at[0]),
                (col_transfer_hbm, transfers.at[1]),
                (leaf_blocks_hbm, leaf_blocks),
                (root_blocks_hbm, root_blocks),
            ]
        )
    ]
    for copy in copies:
        copy.start()
    barrier = pltpu.get_barrier_semaphore()

    def greet(axis, size, place):
        def step(k, carry):
            pl.semaphore_signal(
                barrier, inc=1, device_id={axis: lax.rem(place + k, size)}, device_id_type=MESH
            )
            return carry

        lax.fori_loop(1, size, step, 0)

    greet("col", N_COL, place_col)
    greet("row", N_ROW, place_row)

    x_place = lax.rem(place_col, N_X)
    y_place = lax.div(place_col, N_X)
    always = place_row >= 0
    x_peer = lambda p: {"col": y_place * N_X + p}
    y_peer = lambda p: {"col": p * N_X}
    z_peer = lambda p: {"row": jnp.int32(p)}
    layout = (
        (
            (x_place, always, x_peer),
            (y_place, x_place == 0, y_peer),
            (place_row, place_col == 0, z_peer),
        ),
        (
            (place_row, always, z_peer),
            (x_place, place_row == 0, x_peer),
            (y_place, (place_row == 0) & (x_place == 0), y_peer),
        ),
    )
    stages = []
    for tree in range(2):
        stages.append([])
        for n in range(3):
            at = 7 * (3 * tree + n)
            stages[tree].append(Stage(STAGES[tree][n], *layout[tree][n], stage_refs[at : at + 7]))

    copies[2].wait()
    copies[3].wait()
    for tree in range(2):

        def lay_out(m, carry, tree=tree):
            rows = transfers[tree, pl.ds(lax.div(m, 8) * 256 + lax.rem(m, 8), 32, stride=8), :]
            place = natural.at[tree * 32 + m]
            place[pl.ds(0, 32, stride=2), :] = rows
            place[pl.ds(1, 32, stride=2), :] = pltpu.roll(rows, RANK, 1)
            return carry

        lax.fori_loop(0, 32, lay_out, 0, unroll=4)

    def transfer_of(tree, m):
        return natural[tree * 32 + m][:, :RANK]

    for tree in range(2):
        inner_own[tree] = pack(transfer_of(tree, 31))
    pl.semaphore_wait(barrier, N_COL + N_ROW - 2)
    for tree in range(2):
        for n in range(3):
            stages[tree][n].send_inner(inner_own.at[tree])

    copies[0].wait()
    copies[1].wait()

    def leaf_gram(leaf, carry):
        for tree in range(2):
            rows = bases[tree, pl.ds(lax.div(leaf, 8) * 256 + lax.rem(leaf, 8), 32, stride=8), :]
            basis = unpack(rows)
            grams[tree * GROUP + leaf, :, :RANK] = product_tn(basis, basis)
        return carry

    lax.fori_loop(0, LEAF_DEV, leaf_gram, 0, unroll=4)

    orders = (row_order, col_order)

    def first_level(q, carry):
        for tree in range(2):
            total = None
            for child in range(2):
                leaf = orders[tree][2 * q + child]
                term = sandwich(grams[tree * GROUP + leaf][:, :RANK], transfer_of(tree, leaf))
                total = term if total is None else total + term
            nodes[tree * 16 + q, :, :RANK] = total
        return carry

    lax.fori_loop(0, 8, first_level, 0, unroll=2)
    source, target, offset, count = 0, 8, 16, 8
    while count > 1:
        for tree in range(2):
            for q in range(count // 2):
                total = None
                for child in range(2):
                    node = 2 * q + child
                    term = sandwich(
                        nodes[tree * 16 + source + node][:, :RANK], transfer_of(tree, offset + node)
                    )
                    total = term if total is None else total + term
                if count > 2:
                    nodes[tree * 16 + target + q, :, :RANK] = total
                else:
                    grams[tree * GROUP + LEAF_DEV, :, :RANK] = total
        offset += count
        source, target, count = target, target + count // 2, count // 2

    for tree in range(2):
        stage = stages[tree][0]
        stage.receive_inner()
        stage.make_terms(grams[tree * GROUP + LEAF_DEV][:, :RANK], transfer_of(tree, 30))
        stage.send_terms()

    to_lanes(grams, batch, BATCH)
    factor(batch)
    from_lanes(batch, factors, (GROUP, GROUP))
    row_own[...] = pack(factors[LEAF_DEV * RANK : (LEAF_DEV + 1) * RANK, :RANK])
    col_own[...] = pack(factors[(GROUP + LEAF_DEV) * RANK : (GROUP + LEAF_DEV + 1) * RANK, RANK:])
    row_table[place_col] = row_own[...]
    col_table[place_row] = col_own[...]

    def table_copy(axis, size, place, own, table, sent, got, k, slot):
        return pltpu.make_async_remote_copy(
            own,
            table.at[slot],
            sent.at[k],
            got.at[slot],
            device_id={axis: lax.rem(place + k, size)},
            device_id_type=MESH,
        )

    row_parts = ("col", N_COL, place_col, row_own, row_table, row_sent, row_got)
    col_parts = ("row", N_ROW, place_row, col_own, col_table, col_sent, col_got)
    for parts in (row_parts, col_parts):

        def send(k, carry, parts=parts):
            table_copy(*parts, k, parts[2]).start()
            return carry

        lax.fori_loop(1, parts[1], send, 0)

    for leaf in range(LEAF_DEV):
        leaf_left[leaf] = table_entry(factors[leaf * RANK : (leaf + 1) * RANK, :RANK])
        leaf_right[leaf] = table_entry(factors[(GROUP + leaf) * RANK : (GROUP + leaf + 1) * RANK, RANK:])

    def climb(n):
        for tree in range(2):
            stages[tree][n - 1].receive_terms(highest.at[tree])
            stage = stages[tree][n]
            stage.receive_inner()

            @pl.when(stage.taking_part)
            def _(stage=stage, tree=tree, n=n):
                exit_transfer = unpack(stages[tree][n - 1].inner[stages[tree][n - 1].depth - 1])
                stage.make_terms(unpack(highest[tree]), exit_transfer)

            stage.send_terms()

    climb(1)
    copies[4].wait()
    couple(
        LEAF_PAIRS,
        leaf_blocks,
        block_stage,
        leaf_left,
        leaf_right,
        lambda pair: leaf_pattern[pair],
        lambda pair: leaf_pattern[LEAF_PAIRS + pair],
        leaf_out,
    )
    climb(2)

    for parts in (row_parts, col_parts):

        def receive(k, carry, parts=parts):
            size, place = parts[1], parts[2]
            table_copy(*parts, k, lax.rem(place + size - k, size)).wait_recv()
            return carry

        lax.fori_loop(1, parts[1], receive, 0)

    def convert(table, entries, count):
        def step(n, carry):
            entries[n] = table_entry(unpack(table[n]))
            return carry

        lax.fori_loop(0, count, step, 0, unroll=4)

    convert(row_table, root_left, N_COL)
    convert(col_table, root_right, N_ROW)
    copies[5].wait()
    couple(
        ROOT_PAIRS,
        root_blocks,
        block_stage,
        root_left,
        root_right,
        lambda pair: root_rows[pair],
        lambda pair: root_cols[pair],
        root_out,
    )

    for tree in range(2):
        stages[tree][2].receive_terms(highest.at[tree])
        grams[tree, :, :RANK] = unpack(highest[tree])
    to_lanes(grams, batch, 8)
    factor(batch)
    from_lanes(batch, factors, (8,))
    for tree, out in enumerate((row_out, col_out)):
        out[...] = pack(factors[tree * RANK : (tree + 1) * RANK, RANK:])

    for tree in range(2):
        for n in range(3):
            stages[tree][n].finish()
    for parts in (row_parts, col_parts):

        def drain(k, carry, parts=parts):
            table_copy(*parts, k, parts[2]).wait_send()
            return carry

        lax.fori_loop(1, parts[1], drain, 0)


def tiled(array, rows):
    return array.reshape(rows // 8, 8, 32, 128).transpose(0, 2, 1, 3).reshape(rows * 32, 128)


def untiled(array, rows):
    return array.reshape(rows // 8, 32, 8, 128).transpose(0, 2, 1, 3).reshape(1, rows, RANK * RANK)


def body(
    row_bases,
    col_bases,
    row_transfer,
    col_transfer,
    row_order,
    col_order,
    leaf_pattern,
    leaf_blocks,
    root_rows,
    root_cols,
    root_blocks,
):
    vmem, smem, anywhere = pltpu.VMEM, pltpu.SMEM, pl.ANY
    dma = pltpu.SemaphoreType.DMA
    packed = (32, 128)
    scratch = [
        vmem((2, 512, 128), F32),
        vmem((2, 1024, 128), F32),
        vmem((2048, 128), BF16),
        vmem((1024, 128), BF16),
        dma((6,)),
        vmem((2 * 32, RANK, 128), F32),
        vmem((BATCH, RANK, 128), F32),
        vmem((2 * 16, RANK, 128), F32),
        vmem((RANK, RANK, 128), F32),
        vmem((BATCH * RANK, 128), F32),
        vmem((LEAF_DEV, 2 * RANK, RANK), BF16),
        vmem((LEAF_DEV, 2 * RANK, RANK), BF16),
        vmem((N_COL, 2 * RANK, RANK), BF16),
        vmem((N_ROW, 2 * RANK, RANK), BF16),
        vmem((256, 128), F32),
        vmem((2, *packed), F32),
        vmem((2, *packed), F32),
        vmem(packed, F32),
        vmem(packed, F32),
        vmem((N_COL, *packed), F32),
        vmem((N_ROW, *packed), F32),
        dma((N_COL,)),
        dma((N_COL,)),
        dma((N_ROW,)),
        dma((N_ROW,)),
    ]
    for tree in range(2):
        for depth in STAGES[tree]:
            size = 1 << depth
            scratch += [
                vmem((depth, *packed), F32),
                vmem((depth, *packed), F32),
                vmem((size, *packed), F32),
                dma((size,)),
                dma((depth,)),
                dma((size,)),
                dma((size,)),
            ]
    leaf_out, root_out, row_out, col_out = pl.pallas_call(
        kernel,
        out_shape=(
            jax.ShapeDtypeStruct((LEAF_PAIRS * 32, 128), F32),
            jax.ShapeDtypeStruct((ROOT_PAIRS * 32, 128), F32),
            jax.ShapeDtypeStruct(packed, F32),
            jax.ShapeDtypeStruct(packed, F32),
        ),
        in_specs=[pl.BlockSpec(memory_space=smem)] * 5 + [pl.BlockSpec(memory_space=anywhere)] * 6,
        out_specs=(pl.BlockSpec(memory_space=vmem),) * 4,
        scratch_shapes=scratch,
        compiler_params=pltpu.CompilerParams(
            collective_id=0, has_side_effects=True, vmem_limit_bytes=40 * 2**20
        ),
    )(
        row_order.reshape(LEAF_DEV),
        col_order.reshape(LEAF_DEV),
        leaf_pattern.reshape(2 * LEAF_PAIRS),
        root_rows.reshape(ROOT_PAIRS),
        root_cols.reshape(ROOT_PAIRS),
        tiled(row_bases, LEAF_DEV),
        tiled(col_bases, LEAF_DEV),
        tiled(row_transfer, 2 * LEAF_DEV),
        tiled(col_transfer, 2 * LEAF_DEV),
        tiled(leaf_blocks, LEAF_PAIRS),
        tiled(root_blocks, ROOT_PAIRS),
    )
    return (
        untiled(leaf_out, LEAF_PAIRS),
        untiled(root_out, ROOT_PAIRS),
        row_out.reshape(1, 1, RANK * RANK),
        col_out.reshape(1, 1, RANK * RANK),
    )


def solution(mesh):
    return jax.shard_map(
        body,
        mesh=mesh,
        in_specs=(
            P("row", "col", None),
            P("col", "row", None),
            P("row", "col", None),
            P("col", "row", None),
            P("row", "col", None),
            P("col", "row", None),
            P("row", "col", None),
            P("row", "col", None),
            P("row", "col", None),
            P("row", "col", None),
            P("row", "col", None),
        ),
        out_specs=(
            P("row", "col", None),
            P("row", "col", None),
            P("row", "col", None),
            P("col", "row", None),
        ),
        check_vma=False,
    )
```

```python
import functools

import jax
import jax.numpy as jnp
from jax import lax
from jax.experimental import pallas as pl
from jax.experimental.pallas import tpu as pltpu
from jax.sharding import PartitionSpec as P

RANK = 64
LEAF_DEV = 16
LEAF_PAIRS = 64
ROOT_PAIRS = 32
N_ROW = 16
N_COL = 32
N_X = 4
N_Y = 8
GROUP = 24
BATCH = 2 * GROUP
MESH = pl.DeviceIdType.MESH
F32 = jnp.float32
BF16 = jnp.bfloat16


def split(value):
    high = value.astype(BF16)
    return high, (value - high.astype(F32)).astype(BF16)


def contract(left, right, left_dim, right_dim):
    return lax.dot_general(
        left, right, (((left_dim,), (right_dim,)), ((), ())), preferred_element_type=F32
    )


def product_tn(left, right):
    left_high, left_low = split(left)
    right_high, right_low = split(right)
    return contract(
        jnp.concatenate([left_high, left_high, left_low], 0),
        jnp.concatenate([right_high, right_low, right_high], 0),
        0,
        0,
    )


def product_nn(left, right):
    left_high, left_low = split(left)
    right_high, right_low = split(right)
    both = contract(jnp.concatenate([left_high, left_low], 0), right_high, 1, 0)
    rows = left.shape[0]
    return both[:rows] + both[rows:] + contract(left_high, right_low, 1, 0)


def sandwich(gram, transfer):
    return product_tn(transfer, product_nn(gram, transfer))


def pack(square):
    return jnp.concatenate([square[:32, :], square[32:, :]], 1)


def unpack(packed):
    return jnp.concatenate([packed[:, :RANK], packed[:, RANK:]], 0)


def level_of(place, depth):
    level = jnp.int32(depth)
    for k in range(depth - 1, 0, -1):
        level = jnp.where(lax.rem(place, 1 << k) == 1 << (k - 1), jnp.int32(k), level)
    return level


def span_of(place, depth):
    span = jnp.int32(1 << depth)
    for k in range(depth - 1, 0, -1):
        span = jnp.where(lax.rem(place, 1 << k) == 1 << (k - 1), jnp.int32(1 << k), span)
    return span


def fixed_level(place, depth):
    return depth if place == 0 else (place & -place).bit_length()


class Stage:
    def __init__(self, depth, place, taking_part, peer, refs):
        self.depth, self.size, self.place = depth, 1 << depth, place
        self.taking_part, self.peer = taking_part, peer
        (self.inner, self.terms, self.slots, self.inner_sent, self.inner_got, self.sent, self.got) = refs
        self.level = level_of(place, depth)
        self.span = span_of(place, depth)

    def inner_copy(self, target, level):
        return pltpu.make_async_remote_copy(
            self.own_inner,
            self.inner.at[level - 1],
            self.inner_sent.at[target],
            self.inner_got.at[level - 1],
            device_id=self.peer(target),
            device_id_type=MESH,
        )

    def each_inner_target(self, act):
        for target in range(self.size):
            same = lax.div(self.place, self.span) == lax.div(jnp.int32(target), self.span)
            wanted = (self.place != 0) & (self.place != target) & same
            if target != 0:
                wanted = wanted & (self.span < self.size)
            pl.when(self.taking_part & wanted)(functools.partial(act, target))

    def send_inner(self, own_inner):
        self.own_inner = own_inner
        self.each_inner_target(lambda target: self.inner_copy(target, self.level).start())

    def receive_inner(self):
        for level in range(1, self.depth + 1):
            half = 1 << (level - 1)
            if level < self.depth:
                mine = lax.rem(self.place, 2 * half) == half
                away = jnp.logical_not(mine)

                @pl.when(self.taking_part & mine)
                def _(level=level):
                    self.inner[level - 1] = self.own_inner[...]
            else:
                away = self.place == 0

            @pl.when(self.taking_part & away)
            def _(level=level):
                self.inner_copy(0, level).wait_recv()

    def make_terms(self, gram, transfer):
        path = transfer
        for level in range(1, self.depth + 1):
            self.terms[level - 1] = pack(sandwich(gram, path))
            if level < self.depth:
                path = product_nn(path, unpack(self.inner[level - 1]))

    def term_copy(self, target, sender):
        return pltpu.make_async_remote_copy(
            self.terms.at[fixed_level(target, self.depth) - 1],
            self.slots.at[sender],
            self.sent.at[target],
            self.got.at[sender],
            device_id=self.peer(target),
            device_id_type=MESH,
        )

    def each_target(self, act):
        for target in range(self.size):
            span = 1 << fixed_level(target, self.depth)
            wanted = (self.place != target) & (lax.div(self.place, span) == target // span)
            pl.when(self.taking_part & wanted)(functools.partial(act, target))

    def send_terms(self):
        self.each_target(lambda target: self.term_copy(target, self.place).start())

    def receive_terms(self, total_ref):
        @pl.when(self.taking_part)
        def _():
            total_ref[...] = self.terms[self.level - 1]

        for sender in range(self.size):
            same = lax.div(self.place, self.span) == lax.div(jnp.int32(sender), self.span)

            @pl.when(self.taking_part & (self.place != sender) & same)
            def _(sender=sender):
                self.term_copy(0, sender).wait_recv()
                total_ref[...] += self.slots[sender]

    def finish(self):
        self.each_inner_target(lambda target: self.inner_copy(target, self.level).wait_send())
        self.each_target(lambda target: self.term_copy(target, self.place).wait_send())


def to_lanes(gram_ref, batch_ref, count):
    flat = gram_ref.reshape(gram_ref.shape[0] * RANK, 128)

    def step(j, carry):
        rows = flat[pl.ds(j, count, stride=RANK), :]
        batch_ref[j, :, :count] = rows.T[:RANK, :]
        return carry

    lax.fori_loop(0, RANK, step, 0, unroll=8)


def factor(batch_ref):
    def diagonal(block):
        first, span = 8 * block, slice(8 * block, 8 * block + 8)
        columns = [batch_ref[first + c, span, :] for c in range(8)]
        inverses = []

        def step(c):
            inverse = lax.rsqrt(jnp.broadcast_to(columns[c][c : c + 1, :], (8, 128)))
            column = columns[c] * inverse
            batch_ref[first + c, span, :] = column
            inverses.append(inverse)
            for later in range(c + 1, 8):
                columns[later] = columns[later] - column * column[later : later + 1, :]

        return [functools.partial(step, c) for c in range(8)], inverses

    def below(block, other, inverses):
        first, span = 8 * block, slice(8 * other, 8 * other + 8)
        done = []
        for c in range(8):
            column = batch_ref[first + c, span, :]
            for k in range(c):
                column = column - done[k] * batch_ref[first + k, first + c : first + c + 1, :]
            column = column * inverses[c]
            batch_ref[first + c, span, :] = column
            done.append(column)

    def update(block, j, low, high):
        first, span = 8 * block, slice(8 * low, 8 * high)
        total = batch_ref[j, span, :]
        for c in range(8):
            total = total - batch_ref[first + c, span, :] * batch_ref[first + c, j : j + 1, :]
        batch_ref[j, span, :] = total

    steps, inverses = diagonal(0)
    for step in steps:
        step()
    for block in range(7):
        after = block + 1
        below(block, after, inverses)
        for j in range(8 * after, 8 * after + 8):
            update(block, j, after, after + 1)
        pieces = [functools.partial(below, block, other, inverses) for other in range(after + 1, 8)]
        if after < 7:
            pieces += [functools.partial(update, block, j, after + 1, 8) for j in range(8 * after, 8 * after + 8)]
        pieces += [functools.partial(update, block, j, j // 8, 8) for j in range(8 * after + 8, RANK)]
        steps, inverses = diagonal(after)
        for n, step in enumerate(steps):
            step()
            for piece in pieces[n * len(pieces) // 8 : (n + 1) * len(pieces) // 8]:
                piece()


def from_lanes(batch_ref, factor_ref, counts):
    place = lax.broadcasted_iota(jnp.int32, (RANK, 128), 0)
    first_group = lax.broadcasted_iota(jnp.int32, (RANK, 128), 1) < counts[0]
    halved = jnp.where(place < 32, 2 * place, 2 * place - 63)
    column = jnp.where(first_group, halved, place)

    def step(j, carry):
        plane = batch_ref.at[j]
        halves = jnp.concatenate([plane[pl.ds(0, 32, stride=2), :], plane[pl.ds(1, 32, stride=2), :]], 0)
        values = jnp.where(first_group, halves, plane[...])
        values = jnp.where(column >= j, values, 0.0).T
        moved = lax.div(j, 2) + 32 * lax.rem(j, 2)
        factor_ref[pl.ds(moved, counts[0], stride=RANK), :RANK] = values[: counts[0]]
        factor_ref[pl.ds(counts[0] * RANK + j, counts[1], stride=RANK), :RANK] = values[counts[0] : sum(counts)]
        return carry

    lax.fori_loop(0, RANK, step, 0, unroll=4)


def upper_from_lanes(batch_ref, factor_ref):
    place = lax.broadcasted_iota(jnp.int32, (RANK, 128), 0)

    def step(j, carry):
        values = jnp.where(place >= j, batch_ref[j], 0.0).T
        moved = lax.div(j, 2) + 32 * lax.rem(j, 2)
        factor_ref[pl.ds(moved, 8, stride=RANK), :RANK] = values[:8]
        return carry

    lax.fori_loop(0, RANK, step, 0, unroll=4)


def couple(count, blocks_ref, stage_ref, left_ref, right_ref, left_pick, right_pick, out_ref):
    def step(group, carry):
        base = pl.multiple_of(group * 256, 256)
        stage_ref[...] = blocks_ref[pl.ds(base, 256), :].astype(F32)
        for pair in range(8):
            packed = stage_ref[pl.ds(pair, 32, stride=8), :].astype(BF16)
            square = unpack(packed)
            left = left_ref[left_pick(group * 8 + pair)]
            right = right_ref[right_pick(group * 8 + pair)]
            both = contract(left, square, 1, 0)
            high, low = split(both[:RANK] + both[RANK:])
            out = contract(jnp.concatenate([high, low], 0), right[:RANK], 1, 1)
            out = out[:RANK] + out[RANK:] + contract(high, right[RANK:], 1, 1)
            out_ref[pl.ds(base + pair, 32, stride=8), :] = pack(out)
        return carry

    lax.fori_loop(0, count // 8, step, 0)


def table_entry(value):
    return jnp.concatenate(split(value), 0)


STAGES = ((2, 3, 4), (4, 2, 3))


def kernel(
    row_order_hbm,
    col_order_hbm,
    leaf_pattern_hbm,
    row_bases_hbm,
    col_bases_hbm,
    row_transfer_hbm,
    col_transfer_hbm,
    leaf_blocks_hbm,
    leaf_hbm,
    highest_hbm,
    row_table,
    col_table,
    leaf_out,
    stores,
    row_order,
    col_order,
    leaf_pattern,
    bases,
    transfers,
    leaf_blocks,
    loads,
    natural,
    grams,
    nodes,
    batch,
    factors,
    leaf_left,
    leaf_right,
    block_stage,
    inner_own,
    highest,
    row_own,
    col_own,
    row_sent,
    row_got,
    col_sent,
    col_got,
    *stage_refs,
):
    place_row = lax.axis_index("row")
    place_col = lax.axis_index("col")
    copies = [
        pltpu.make_async_copy(source, target, loads.at[n])
        for n, (source, target) in enumerate(
            [
                (row_transfer_hbm, transfers.at[0]),
                (col_transfer_hbm, transfers.at[1]),
                (row_bases_hbm, bases.at[0]),
                (col_bases_hbm, bases.at[1]),
                (row_order_hbm, row_order),
                (col_order_hbm, col_order),
                (leaf_blocks_hbm, leaf_blocks),
                (leaf_pattern_hbm, leaf_pattern),
            ]
        )
    ]
    for copy in copies:
        copy.start()
    leaf_store, highest_store, row_keep, col_keep = (
        pltpu.make_async_copy(source, target, stores.at[n])
        for n, (source, target) in enumerate(
            [
                (leaf_out, leaf_hbm),
                (highest, highest_hbm),
                (row_own, row_table.at[place_col]),
                (col_own, col_table.at[place_row]),
            ]
        )
    )
    barrier = pltpu.get_barrier_semaphore()

    def greet(axis, size, place):
        def step(k, carry):
            pl.semaphore_signal(
                barrier, inc=1, device_id={axis: lax.rem(place + k, size)}, device_id_type=MESH
            )
            return carry

        lax.fori_loop(1, size, step, 0)

    greet("col", N_COL, place_col)
    greet("row", N_ROW, place_row)

    x_place = lax.rem(place_col, N_X)
    y_place = lax.div(place_col, N_X)
    always = place_row >= 0
    x_peer = lambda p: {"col": y_place * N_X + p}
    y_peer = lambda p: {"col": p * N_X}
    z_peer = lambda p: {"row": jnp.int32(p)}
    layout = (
        (
            (x_place, always, x_peer),
            (y_place, x_place == 0, y_peer),
            (place_row, place_col == 0, z_peer),
        ),
        (
            (place_row, always, z_peer),
            (x_place, place_row == 0, x_peer),
            (y_place, (place_row == 0) & (x_place == 0), y_peer),
        ),
    )
    stages = []
    for tree in range(2):
        stages.append([])
        for n in range(3):
            at = 7 * (3 * tree + n)
            stages[tree].append(Stage(STAGES[tree][n], *layout[tree][n], stage_refs[at : at + 7]))

    for copy in copies[:2]:
        copy.wait()
    for tree in range(2):

        def lay_out(m, carry, tree=tree):
            rows = transfers[tree, pl.ds(lax.div(m, 8) * 256 + lax.rem(m, 8), 32, stride=8), :]
            place = natural.at[tree * 32 + m]
            place[pl.ds(0, 32, stride=2), :] = rows
            place[pl.ds(1, 32, stride=2), :] = pltpu.roll(rows, RANK, 1)
            return carry

        lax.fori_loop(0, 32, lay_out, 0, unroll=4)

    def transfer_of(tree, m):
        return natural[tree * 32 + m][:, :RANK]

    for tree in range(2):
        inner_own[tree] = pack(transfer_of(tree, 31))
    pl.semaphore_wait(barrier, N_COL + N_ROW - 2)
    for tree in range(2):
        for n in range(3):
            stages[tree][n].send_inner(inner_own.at[tree])

    for copy in copies[2:6]:
        copy.wait()

    def leaf_gram(leaf, carry):
        for tree in range(2):
            rows = bases[tree, pl.ds(lax.div(leaf, 8) * 256 + lax.rem(leaf, 8), 32, stride=8), :]
            basis = unpack(rows)
            grams[tree * GROUP + leaf, :, :RANK] = product_tn(basis, basis)
        return carry

    lax.fori_loop(0, LEAF_DEV, leaf_gram, 0, unroll=4)

    orders = (row_order, col_order)

    def first_level(q, carry):
        for tree in range(2):
            total = None
            for child in range(2):
                leaf = orders[tree][0, 0, 2 * q + child]
                term = sandwich(grams[tree * GROUP + leaf][:, :RANK], transfer_of(tree, leaf))
                total = term if total is None else total + term
            nodes[tree * 16 + q, :, :RANK] = total
        return carry

    lax.fori_loop(0, 8, first_level, 0, unroll=2)
    source, target, offset, count = 0, 8, 16, 8
    while count > 1:
        for tree in range(2):
            for q in range(count // 2):
                total = None
                for child in range(2):
                    node = 2 * q + child
                    term = sandwich(
                        nodes[tree * 16 + source + node][:, :RANK], transfer_of(tree, offset + node)
                    )
                    total = term if total is None else total + term
                if count > 2:
                    nodes[tree * 16 + target + q, :, :RANK] = total
                else:
                    grams[tree * GROUP + LEAF_DEV, :, :RANK] = total
        offset += count
        source, target, count = target, target + count // 2, count // 2

    for tree in range(2):
        stage = stages[tree][0]
        stage.receive_inner()
        stage.make_terms(grams[tree * GROUP + LEAF_DEV][:, :RANK], transfer_of(tree, 30))
        stage.send_terms()

    to_lanes(grams, batch, BATCH)
    factor(batch)
    from_lanes(batch, factors, (GROUP, GROUP))
    row_own[...] = pack(factors[LEAF_DEV * RANK : (LEAF_DEV + 1) * RANK, :RANK])
    col_own[...] = pack(factors[(GROUP + LEAF_DEV) * RANK : (GROUP + LEAF_DEV + 1) * RANK, :RANK])
    row_keep.start()
    col_keep.start()

    def table_copy(axis, size, place, own, table, sent, got, k, slot):
        return pltpu.make_async_remote_copy(
            own,
            table.at[slot],
            sent.at[k],
            got.at[slot],
            device_id={axis: lax.rem(place + k, size)},
            device_id_type=MESH,
        )

    row_parts = ("col", N_COL, place_col, row_own, row_table, row_sent, row_got)
    col_parts = ("row", N_ROW, place_row, col_own, col_table, col_sent, col_got)
    for parts in (row_parts, col_parts):

        def send(k, carry, parts=parts):
            table_copy(*parts, k, parts[2]).start()
            return carry

        lax.fori_loop(1, parts[1], send, 0)

    for leaf in range(LEAF_DEV):
        leaf_left[leaf] = table_entry(factors[leaf * RANK : (leaf + 1) * RANK, :RANK])
        leaf_right[leaf] = table_entry(factors[(GROUP + leaf) * RANK : (GROUP + leaf + 1) * RANK, :RANK])

    def climb(n):
        for tree in range(2):
            stages[tree][n - 1].receive_terms(highest.at[tree])
            stage = stages[tree][n]
            stage.receive_inner()

            @pl.when(stage.taking_part)
            def _(stage=stage, tree=tree, n=n):
                exit_transfer = unpack(stages[tree][n - 1].inner[stages[tree][n - 1].depth - 1])
                stage.make_terms(unpack(highest[tree]), exit_transfer)

            stage.send_terms()

    climb(1)
    for copy in copies[6:8]:
        copy.wait()
    couple(
        LEAF_PAIRS,
        leaf_blocks,
        block_stage,
        leaf_left,
        leaf_right,
        lambda pair: leaf_pattern[0, 0, pair],
        lambda pair: leaf_pattern[0, 1, pair],
        leaf_out,
    )
    leaf_store.start()
    climb(2)

    for tree in range(2):
        stages[tree][2].receive_terms(highest.at[tree])
    highest_store.start()
    for parts in (row_parts, col_parts):

        def receive(k, carry, parts=parts):
            size, place = parts[1], parts[2]
            table_copy(*parts, k, lax.rem(place + size - k, size)).wait_recv()
            return carry

        lax.fori_loop(1, parts[1], receive, 0)

    for tree in range(2):
        for n in range(3):
            stages[tree][n].finish()
    for parts in (row_parts, col_parts):

        def drain(k, carry, parts=parts):
            table_copy(*parts, k, parts[2]).wait_send()
            return carry

        lax.fori_loop(1, parts[1], drain, 0)
    for store in (leaf_store, highest_store, row_keep, col_keep):
        store.wait()


def finish(
    leaf_hbm,
    highest_hbm,
    row_table_hbm,
    col_table_hbm,
    root_rows_hbm,
    root_cols_hbm,
    root_blocks_hbm,
    leaf_end,
    root_end,
    row_end,
    col_end,
    leaf_pass,
    highest,
    row_table,
    col_table,
    root_rows,
    root_cols,
    root_blocks,
    root_out,
    row_out,
    col_out,
    loads,
    stores,
    grams,
    batch,
    factors,
    root_left,
    root_right,
    block_stage,
):
    copies = [
        pltpu.make_async_copy(source, target, loads.at[n])
        for n, (source, target) in enumerate(
            [
                (highest_hbm, highest),
                (leaf_hbm, leaf_pass),
                (row_table_hbm, row_table),
                (col_table_hbm, col_table),
                (root_rows_hbm, root_rows),
                (root_cols_hbm, root_cols),
                (root_blocks_hbm, root_blocks),
            ]
        )
    ]
    for copy in copies:
        copy.start()
    results = [
        pltpu.make_async_copy(source, target, stores.at[n])
        for n, (source, target) in enumerate(
            [(leaf_pass, leaf_end), (row_out, row_end), (col_out, col_end), (root_out, root_end)]
        )
    ]
    copies[0].wait()
    for tree in range(2):
        grams[tree, :, :RANK] = unpack(highest[tree])
    to_lanes(grams, batch, 8)
    factor(batch)
    copies[1].wait()
    results[0].start()
    upper_from_lanes(batch, factors)
    for tree, out in enumerate((row_out, col_out)):
        out[...] = pack(factors[tree * RANK : (tree + 1) * RANK, :RANK])
    results[1].start()
    results[2].start()

    for copy in copies[2:]:
        copy.wait()

    def convert(table, entries, count):
        def step(n, carry):
            entries[n] = table_entry(unpack(table[n]))
            return carry

        lax.fori_loop(0, count, step, 0, unroll=4)

    convert(row_table, root_left, N_COL)
    convert(col_table, root_right, N_ROW)
    couple(
        ROOT_PAIRS,
        root_blocks,
        block_stage,
        root_left,
        root_right,
        lambda pair: root_rows[0, 0, pair],
        lambda pair: root_cols[0, 0, pair],
        root_out,
    )
    results[3].start()
    for result in results:
        result.wait()


def tiled(array, rows):
    return array.reshape(rows // 8, 8, 32, 128).transpose(0, 2, 1, 3).reshape(rows * 32, 128)


def untiled(array, rows):
    return array.reshape(rows // 8, 32, 8, 128).transpose(0, 2, 1, 3).reshape(1, rows, RANK * RANK)


def body(
    row_bases,
    col_bases,
    row_transfer,
    col_transfer,
    row_order,
    col_order,
    leaf_pattern,
    leaf_blocks,
    root_rows,
    root_cols,
    root_blocks,
):
    vmem, smem = pltpu.VMEM, pltpu.SMEM
    dma = pltpu.SemaphoreType.DMA
    hbm = pl.BlockSpec(memory_space=pltpu.HBM)
    shape = jax.ShapeDtypeStruct
    packed = (32, 128)
    scratch = [
        vmem((LEAF_PAIRS * 32, 128), F32),
        dma((4,)),
        smem((1, 1, LEAF_DEV), jnp.int32),
        smem((1, 1, LEAF_DEV), jnp.int32),
        smem((1, 2, LEAF_PAIRS), jnp.int32),
        vmem((2, 512, 128), F32),
        vmem((2, 1024, 128), F32),
        vmem((2048, 128), BF16),
        dma((8,)),
        vmem((2 * 32, RANK, 128), F32),
        vmem((BATCH, RANK, 128), F32),
        vmem((2 * 16, RANK, 128), F32),
        vmem((RANK, RANK, 128), F32),
        vmem((BATCH * RANK, 128), F32),
        vmem((LEAF_DEV, 2 * RANK, RANK), BF16),
        vmem((LEAF_DEV, 2 * RANK, RANK), BF16),
        vmem((256, 128), F32),
        vmem((2, *packed), F32),
        vmem((2, *packed), F32),
        vmem(packed, F32),
        vmem(packed, F32),
        dma((N_COL,)),
        dma((N_COL,)),
        dma((N_ROW,)),
        dma((N_ROW,)),
    ]
    for tree in range(2):
        for depth in STAGES[tree]:
            size = 1 << depth
            scratch += [
                vmem((depth, *packed), F32),
                vmem((depth, *packed), F32),
                vmem((size, *packed), F32),
                dma((size,)),
                dma((depth,)),
                dma((size,)),
                dma((size,)),
            ]
    parts = pl.pallas_call(
        kernel,
        out_shape=(
            shape((LEAF_PAIRS * 32, 128), F32),
            shape((2, *packed), F32),
            shape((N_COL, *packed), F32),
            shape((N_ROW, *packed), F32),
        ),
        in_specs=[hbm] * 8,
        out_specs=(hbm,) * 4,
        scratch_shapes=scratch,
        compiler_params=pltpu.CompilerParams(
            collective_id=0, has_side_effects=True, vmem_limit_bytes=62 * 2**20
        ),
    )(
        row_order,
        col_order,
        leaf_pattern,
        tiled(row_bases, LEAF_DEV),
        tiled(col_bases, LEAF_DEV),
        tiled(row_transfer, 2 * LEAF_DEV),
        tiled(col_transfer, 2 * LEAF_DEV),
        tiled(leaf_blocks, LEAF_PAIRS),
    )
    leaf_out, root_out, row_out, col_out = pl.pallas_call(
        finish,
        out_shape=(
            shape((LEAF_PAIRS * 32, 128), F32),
            shape((ROOT_PAIRS * 32, 128), F32),
            shape(packed, F32),
            shape(packed, F32),
        ),
        in_specs=[hbm] * 7,
        out_specs=(hbm,) * 4,
        scratch_shapes=[
            vmem((LEAF_PAIRS * 32, 128), F32),
            vmem((2, *packed), F32),
            vmem((N_COL, *packed), F32),
            vmem((N_ROW, *packed), F32),
            smem((1, 1, ROOT_PAIRS), jnp.int32),
            smem((1, 1, ROOT_PAIRS), jnp.int32),
            vmem((1024, 128), BF16),
            vmem((ROOT_PAIRS * 32, 128), F32),
            vmem(packed, F32),
            vmem(packed, F32),
            dma((7,)),
            dma((4,)),
            vmem((8, RANK, 128), F32),
            vmem((RANK, RANK, 128), F32),
            vmem((8 * RANK, 128), F32),
            vmem((N_COL, 2 * RANK, RANK), BF16),
            vmem((N_ROW, 2 * RANK, RANK), BF16),
            vmem((256, 128), F32),
        ],
        compiler_params=pltpu.CompilerParams(vmem_limit_bytes=62 * 2**20),
    )(*parts, root_rows, root_cols, tiled(root_blocks, ROOT_PAIRS))
    return (
        untiled(leaf_out, LEAF_PAIRS),
        untiled(root_out, ROOT_PAIRS),
        row_out.reshape(1, 1, RANK * RANK),
        col_out.reshape(1, 1, RANK * RANK),
    )


def solution(mesh):
    return jax.shard_map(
        body,
        mesh=mesh,
        in_specs=(
            P("row", "col", None),
            P("col", "row", None),
            P("row", "col", None),
            P("col", "row", None),
            P("row", "col", None),
            P("col", "row", None),
            P("row", "col", None),
            P("row", "col", None),
            P("row", "col", None),
            P("row", "col", None),
            P("row", "col", None),
        ),
        out_specs=(
            P("row", "col", None),
            P("row", "col", None),
            P("row", "col", None),
            P("col", "row", None),
        ),
        check_vma=False,
    )
```

```python
import functools

import jax
import jax.numpy as jnp
from jax import lax
from jax.experimental import pallas as pl
from jax.experimental.pallas import tpu as pltpu
from jax.sharding import PartitionSpec as P

RANK = 64
LEAF_DEV = 16
LEAF_PAIRS = 64
ROOT_PAIRS = 32
N_ROW = 16
N_COL = 32
N_X = 4
N_Y = 8
N_Z = 8
N_CORE = 2
ROOT_BATCH = N_COL + N_ROW + 8
MESH = pl.DeviceIdType.MESH
F32 = jnp.float32
BF16 = jnp.bfloat16


def split(value):
    high = value.astype(BF16)
    return high, (value - high.astype(F32)).astype(BF16)


def contract(left, right, left_dim, right_dim):
    return lax.dot_general(
        left, right, (((left_dim,), (right_dim,)), ((), ())), preferred_element_type=F32
    )


def product_tn(left, right):
    left_high, left_low = split(left)
    right_high, right_low = split(right)
    return contract(
        jnp.concatenate([left_high, left_high, left_low], 0),
        jnp.concatenate([right_high, right_low, right_high], 0),
        0,
        0,
    )


def product_nn(left, right):
    left_high, left_low = split(left)
    right_high, right_low = split(right)
    both = contract(jnp.concatenate([left_high, left_low], 0), right_high, 1, 0)
    rows = left.shape[0]
    return both[:rows] + both[rows:] + contract(left_high, right_low, 1, 0)


def sandwich(gram, transfer):
    return product_tn(transfer, product_nn(gram, transfer))


def pack(square):
    return jnp.concatenate([square[:32, :], square[32:, :]], 1)


def unpack(packed):
    return jnp.concatenate([packed[:, :RANK], packed[:, RANK:]], 0)


def level_of(place, depth):
    level = jnp.int32(depth)
    for k in range(depth - 1, 0, -1):
        level = jnp.where(lax.rem(place, 1 << k) == 1 << (k - 1), jnp.int32(k), level)
    return level


def span_of(place, depth):
    span = jnp.int32(1 << depth)
    for k in range(depth - 1, 0, -1):
        span = jnp.where(lax.rem(place, 1 << k) == 1 << (k - 1), jnp.int32(1 << k), span)
    return span


def fixed_level(place, depth):
    return depth if place == 0 else (place & -place).bit_length()


class Stage:
    def __init__(self, depth, place, taking_part, peer, refs):
        self.depth, self.size, self.place = depth, 1 << depth, place
        self.taking_part, self.peer = taking_part, peer
        (self.inner, self.terms, self.slots, self.inner_sent, self.inner_got, self.sent, self.got) = refs
        self.level = level_of(place, depth)
        self.span = span_of(place, depth)

    def inner_copy(self, target, level):
        return pltpu.make_async_remote_copy(
            self.own_inner,
            self.inner.at[level - 1],
            self.inner_sent.at[target],
            self.inner_got.at[level - 1],
            device_id=self.peer(target),
            device_id_type=MESH,
        )

    def each_inner_target(self, act):
        for target in range(self.size):
            same = lax.div(self.place, self.span) == lax.div(jnp.int32(target), self.span)
            wanted = (self.place != 0) & (self.place != target) & same
            if target != 0:
                wanted = wanted & (self.span < self.size)
            pl.when(self.taking_part & wanted)(functools.partial(act, target))

    def send_inner(self, own_inner):
        self.own_inner = own_inner
        self.each_inner_target(lambda target: self.inner_copy(target, self.level).start())

    def receive_inner(self):
        for level in range(1, self.depth + 1):
            half = 1 << (level - 1)
            if level < self.depth:
                mine = lax.rem(self.place, 2 * half) == half
                away = jnp.logical_not(mine)

                @pl.when(self.taking_part & mine)
                def _(level=level):
                    self.inner[level - 1] = self.own_inner[...]
            else:
                away = self.place == 0

            @pl.when(self.taking_part & away)
            def _(level=level):
                self.inner_copy(0, level).wait_recv()

    def make_terms(self, gram, transfer):
        path = transfer
        for level in range(1, self.depth + 1):
            self.terms[level - 1] = pack(sandwich(gram, path))
            if level < self.depth:
                path = product_nn(path, unpack(self.inner[level - 1]))

    def term_copy(self, target, sender):
        return pltpu.make_async_remote_copy(
            self.terms.at[fixed_level(target, self.depth) - 1],
            self.slots.at[sender],
            self.sent.at[target],
            self.got.at[sender],
            device_id=self.peer(target),
            device_id_type=MESH,
        )

    def each_target(self, act):
        for target in range(self.size):
            span = 1 << fixed_level(target, self.depth)
            wanted = (self.place != target) & (lax.div(self.place, span) == target // span)
            pl.when(self.taking_part & wanted)(functools.partial(act, target))

    def send_terms(self):
        self.each_target(lambda target: self.term_copy(target, self.place).start())

    def receive_terms(self, total_ref):
        @pl.when(self.taking_part)
        def _():
            total_ref[...] = self.terms[self.level - 1]

        for sender in range(self.size):
            same = lax.div(self.place, self.span) == lax.div(jnp.int32(sender), self.span)

            @pl.when(self.taking_part & (self.place != sender) & same)
            def _(sender=sender):
                self.term_copy(0, sender).wait_recv()
                total_ref[...] += self.slots[sender]

    def finish(self):
        self.each_inner_target(lambda target: self.inner_copy(target, self.level).wait_send())
        self.each_target(lambda target: self.term_copy(target, self.place).wait_send())


def to_lanes(gram_ref, batch_ref, count):
    flat = gram_ref.reshape(gram_ref.shape[0] * RANK, 128)

    def step(j, carry):
        rows = flat[pl.ds(j, count, stride=RANK), :]
        batch_ref[j, :, :count] = rows.T[:RANK, :]
        return carry

    lax.fori_loop(0, RANK, step, 0, unroll=8)


def factor(batch_ref):
    def diagonal(block):
        first, span = 8 * block, slice(8 * block, 8 * block + 8)
        columns = [batch_ref[first + c, span, :] for c in range(8)]
        inverses = []

        def step(c):
            inverse = lax.rsqrt(jnp.broadcast_to(columns[c][c : c + 1, :], (8, 128)))
            column = columns[c] * inverse
            batch_ref[first + c, span, :] = column
            inverses.append(inverse)
            for later in range(c + 1, 8):
                columns[later] = columns[later] - column * column[later : later + 1, :]

        return [functools.partial(step, c) for c in range(8)], inverses

    def below(block, other, inverses):
        first, span = 8 * block, slice(8 * other, 8 * other + 8)
        done = []
        for c in range(8):
            column = batch_ref[first + c, span, :]
            for k in range(c):
                column = column - done[k] * batch_ref[first + k, first + c : first + c + 1, :]
            column = column * inverses[c]
            batch_ref[first + c, span, :] = column
            done.append(column)

    def update(block, j, low, high):
        first, span = 8 * block, slice(8 * low, 8 * high)
        total = batch_ref[j, span, :]
        for c in range(8):
            total = total - batch_ref[first + c, span, :] * batch_ref[first + c, j : j + 1, :]
        batch_ref[j, span, :] = total

    steps, inverses = diagonal(0)
    for step in steps:
        step()
    for block in range(7):
        after = block + 1
        below(block, after, inverses)
        for j in range(8 * after, 8 * after + 8):
            update(block, j, after, after + 1)
        pieces = [functools.partial(below, block, other, inverses) for other in range(after + 1, 8)]
        if after < 7:
            pieces += [functools.partial(update, block, j, after + 1, 8) for j in range(8 * after, 8 * after + 8)]
        pieces += [functools.partial(update, block, j, j // 8, 8) for j in range(8 * after + 8, RANK)]
        steps, inverses = diagonal(after)
        for n, step in enumerate(steps):
            step()
            for piece in pieces[n * len(pieces) // 8 : (n + 1) * len(pieces) // 8]:
                piece()


def from_lanes(batch_ref, factor_ref, counts):
    place = lax.broadcasted_iota(jnp.int32, (RANK, 128), 0)
    first_group = lax.broadcasted_iota(jnp.int32, (RANK, 128), 1) < counts[0]
    halved = jnp.where(place < 32, 2 * place, 2 * place - 63)
    column = jnp.where(first_group, halved, place)

    def step(j, carry):
        plane = batch_ref.at[j]
        halves = jnp.concatenate([plane[pl.ds(0, 32, stride=2), :], plane[pl.ds(1, 32, stride=2), :]], 0)
        values = jnp.where(first_group, halves, plane[...])
        values = jnp.where(column >= j, values, 0.0).T
        moved = lax.div(j, 2) + 32 * lax.rem(j, 2)
        factor_ref[pl.ds(moved, counts[0], stride=RANK), :RANK] = values[: counts[0]]
        factor_ref[pl.ds(counts[0] * RANK + j, counts[1], stride=RANK), :RANK] = values[counts[0] : sum(counts)]
        return carry

    lax.fori_loop(0, RANK, step, 0, unroll=4)


def couple(count, blocks_ref, stage_ref, left_ref, right_ref, left_pick, right_pick, out_ref):
    def step(group, carry):
        base = pl.multiple_of(group * 256, 256)
        stage_ref[...] = blocks_ref[pl.ds(base, 256), :].astype(F32)
        for pair in range(8):
            packed = stage_ref[pl.ds(pair, 32, stride=8), :].astype(BF16)
            square = unpack(packed)
            left = left_ref[left_pick(group * 8 + pair)]
            right = right_ref[right_pick(group * 8 + pair)]
            both = contract(left, square, 1, 0)
            high, low = split(both[:RANK] + both[RANK:])
            out = contract(jnp.concatenate([high, low], 0), right[:RANK], 1, 1)
            out = out[:RANK] + out[RANK:] + contract(high, right[RANK:], 1, 1)
            out_ref[pl.ds(base + pair, 32, stride=8), :] = pack(out)
        return carry

    lax.fori_loop(0, count // 8, step, 0)


def table_entry(value):
    return jnp.concatenate(split(value), 0)


STAGES = ((2, 3, 4), (4, 2, 3))


def kernel(
    row_order_hbm,
    col_order_hbm,
    leaf_pattern_hbm,
    row_bases_hbm,
    col_bases_hbm,
    row_transfer_hbm,
    col_transfer_hbm,
    leaf_blocks_hbm,
    leaf_hbm,
    highest_hbm,
    row_table,
    col_table,
    leaf_out,
    stores,
    row_order,
    col_order,
    leaf_pattern,
    bases,
    transfers,
    leaf_blocks,
    loads,
    natural,
    grams,
    nodes,
    batch,
    factors,
    leaf_left,
    leaf_right,
    block_stage,
    inner_own,
    highest,
    roots,
    root_own,
    root_line,
    line_sent,
    line_got,
    spread_sent,
    spread_got,
    *stage_refs,
):
    place_row = lax.axis_index("row")
    place_col = lax.axis_index("col")
    copies = [
        pltpu.make_async_copy(source, target, loads.at[n])
        for n, (source, target) in enumerate(
            [
                (row_transfer_hbm, transfers.at[0]),
                (col_transfer_hbm, transfers.at[1]),
                (row_bases_hbm, bases.at[0]),
                (col_bases_hbm, bases.at[1]),
                (row_order_hbm, row_order),
                (col_order_hbm, col_order),
                (leaf_blocks_hbm, leaf_blocks),
                (leaf_pattern_hbm, leaf_pattern),
            ]
        )
    ]
    for copy in copies:
        copy.start()
    leaf_store = pltpu.make_async_copy(leaf_out, leaf_hbm, stores.at[0])
    highest_store = pltpu.make_async_copy(highest, highest_hbm, stores.at[1])
    barrier = pltpu.get_barrier_semaphore()

    def greet(axis, size, place):
        def step(k, carry):
            pl.semaphore_signal(
                barrier, inc=1, device_id={axis: lax.rem(place + k, size)}, device_id_type=MESH
            )
            return carry

        lax.fori_loop(1, size, step, 0)

    greet("col", N_COL, place_col)
    greet("row", N_ROW, place_row)

    x_place = lax.rem(place_col, N_X)
    y_place = lax.div(place_col, N_X)
    always = place_row >= 0
    x_peer = lambda p: {"col": y_place * N_X + p}
    y_peer = lambda p: {"col": p * N_X}
    z_peer = lambda p: {"row": jnp.int32(p)}
    z_place = lax.div(place_row, N_CORE)
    core_place = lax.rem(place_row, N_CORE)
    line_places = (y_place, z_place)

    def line_copy(tree, k, slot):
        place = lax.rem(line_places[tree] + k, 8)
        peer = {"col": place * N_X + x_place} if tree == 0 else {"row": place * N_CORE + core_place}
        return pltpu.make_async_remote_copy(
            root_own.at[tree],
            root_line.at[tree, slot],
            line_sent.at[tree, k],
            line_got.at[tree, slot],
            device_id=peer,
            device_id_type=MESH,
        )

    spreads = ((row_table, N_X, x_place), (col_table, N_CORE, core_place))

    def spread_copy(tree, k, slot):
        table, size, place = spreads[tree]
        to = lax.rem(place + k, size)
        peer = {"col": y_place * N_X + to} if tree == 0 else {"row": z_place * N_CORE + to}
        return pltpu.make_async_remote_copy(
            root_line.at[tree],
            table.at[slot],
            spread_sent.at[tree, k],
            spread_got.at[tree, slot],
            device_id=peer,
            device_id_type=MESH,
        )

    spread_copies = [[spread_copy(tree, k, spreads[tree][2]) for k in range(1, spreads[tree][1])] for tree in range(2)]
    keep_copies = [
        pltpu.make_async_copy(root_line.at[tree], spreads[tree][0].at[spreads[tree][2]], stores.at[2 + tree])
        for tree in range(2)
    ]
    layout = (
        (
            (x_place, always, x_peer),
            (y_place, x_place == 0, y_peer),
            (place_row, place_col == 0, z_peer),
        ),
        (
            (place_row, always, z_peer),
            (x_place, place_row == 0, x_peer),
            (y_place, (place_row == 0) & (x_place == 0), y_peer),
        ),
    )
    stages = []
    for tree in range(2):
        stages.append([])
        for n in range(3):
            at = 7 * (3 * tree + n)
            stages[tree].append(Stage(STAGES[tree][n], *layout[tree][n], stage_refs[at : at + 7]))

    for copy in copies[:2]:
        copy.wait()
    for tree in range(2):

        def lay_out(m, carry, tree=tree):
            rows = transfers[tree, pl.ds(lax.div(m, 8) * 256 + lax.rem(m, 8), 32, stride=8), :]
            place = natural.at[tree * 32 + m]
            place[pl.ds(0, 32, stride=2), :] = rows
            place[pl.ds(1, 32, stride=2), :] = pltpu.roll(rows, RANK, 1)
            return carry

        lax.fori_loop(0, 32, lay_out, 0, unroll=4)

    def transfer_of(tree, m):
        return natural[tree * 32 + m][:, :RANK]

    for tree in range(2):
        inner_own[tree] = pack(transfer_of(tree, 31))
    pl.semaphore_wait(barrier, N_COL + N_ROW - 2)
    for tree in range(2):
        for n in range(3):
            stages[tree][n].send_inner(inner_own.at[tree])

    for copy in copies[2:6]:
        copy.wait()

    def leaf_gram(leaf, carry):
        for tree in range(2):
            rows = bases[tree, pl.ds(lax.div(leaf, 8) * 256 + lax.rem(leaf, 8), 32, stride=8), :]
            basis = unpack(rows)
            grams[tree * LEAF_DEV + leaf, :, :RANK] = product_tn(basis, basis)
        return carry

    lax.fori_loop(0, LEAF_DEV, leaf_gram, 0, unroll=4)

    orders = (row_order, col_order)

    def first_level(q, carry):
        for tree in range(2):
            total = None
            for child in range(2):
                leaf = orders[tree][0, 0, 2 * q + child]
                term = sandwich(grams[tree * LEAF_DEV + leaf][:, :RANK], transfer_of(tree, leaf))
                total = term if total is None else total + term
            nodes[tree * 16 + q, :, :RANK] = total
        return carry

    lax.fori_loop(0, 8, first_level, 0, unroll=2)
    source, target, offset, count = 0, 8, 16, 8
    while count > 1:
        for tree in range(2):
            for q in range(count // 2):
                total = None
                for child in range(2):
                    node = 2 * q + child
                    term = sandwich(
                        nodes[tree * 16 + source + node][:, :RANK], transfer_of(tree, offset + node)
                    )
                    total = term if total is None else total + term
                if count > 2:
                    nodes[tree * 16 + target + q, :, :RANK] = total
                else:
                    roots[tree] = total
        offset += count
        source, target, count = target, target + count // 2, count // 2

    for tree in range(2):
        stage = stages[tree][0]
        stage.receive_inner()
        stage.make_terms(roots[tree], transfer_of(tree, 30))
        stage.send_terms()

    for tree in range(2):
        root_own[tree] = pack(roots[tree])
        root_line[tree, line_places[tree]] = root_own[tree]
    for tree in range(2):
        for k in range(1, 8):
            line_copy(tree, k, line_places[tree]).start()

    to_lanes(grams, batch, 2 * LEAF_DEV)
    factor(batch)
    from_lanes(batch, factors, (LEAF_DEV, LEAF_DEV))
    for tree in range(2):
        for k in range(1, 8):
            line_copy(tree, k, lax.rem(line_places[tree] + 8 - k, 8)).wait_recv()
        for copy in keep_copies[tree : tree + 1] + spread_copies[tree]:
            copy.start()
    for leaf in range(LEAF_DEV):
        leaf_left[leaf] = table_entry(factors[leaf * RANK : (leaf + 1) * RANK, :RANK])
        leaf_right[leaf] = table_entry(factors[(LEAF_DEV + leaf) * RANK : (LEAF_DEV + leaf + 1) * RANK, :RANK])

    def climb(n):
        for tree in range(2):
            stages[tree][n - 1].receive_terms(highest.at[tree])
            stage = stages[tree][n]
            stage.receive_inner()

            @pl.when(stage.taking_part)
            def _(stage=stage, tree=tree, n=n):
                exit_transfer = unpack(stages[tree][n - 1].inner[stages[tree][n - 1].depth - 1])
                stage.make_terms(unpack(highest[tree]), exit_transfer)

            stage.send_terms()

    climb(1)
    for copy in copies[6:8]:
        copy.wait()
    couple(
        LEAF_PAIRS,
        leaf_blocks,
        block_stage,
        leaf_left,
        leaf_right,
        lambda pair: leaf_pattern[0, 0, pair],
        lambda pair: leaf_pattern[0, 1, pair],
        leaf_out,
    )
    leaf_store.start()
    climb(2)

    for tree in range(2):
        stages[tree][2].receive_terms(highest.at[tree])
    highest_store.start()
    for tree in range(2):
        for k in range(1, spreads[tree][1]):
            spread_copy(tree, k, lax.rem(spreads[tree][2] + spreads[tree][1] - k, spreads[tree][1])).wait_recv()
    for tree in range(2):
        for n in range(3):
            stages[tree][n].finish()
    for tree in range(2):
        for k in range(1, 8):
            line_copy(tree, k, line_places[tree]).wait_send()
        for copy in spread_copies[tree]:
            copy.wait_send()
    for store in (leaf_store, highest_store, *keep_copies):
        store.wait()


def finish(
    leaf_hbm,
    highest_hbm,
    row_table_hbm,
    col_table_hbm,
    root_rows_hbm,
    root_cols_hbm,
    root_blocks_hbm,
    leaf_end,
    root_end,
    row_end,
    col_end,
    leaf_pass,
    highest,
    row_table,
    col_table,
    root_rows,
    root_cols,
    root_blocks,
    root_out,
    row_out,
    col_out,
    loads,
    stores,
    grams,
    batch,
    factors,
    root_left,
    root_right,
    block_stage,
):
    copies = [
        pltpu.make_async_copy(source, target, loads.at[n])
        for n, (source, target) in enumerate(
            [
                (highest_hbm, highest),
                (leaf_hbm, leaf_pass),
                (row_table_hbm, row_table),
                (col_table_hbm, col_table),
                (root_rows_hbm, root_rows),
                (root_cols_hbm, root_cols),
                (root_blocks_hbm, root_blocks),
            ]
        )
    ]
    for copy in copies:
        copy.start()
    results = [
        pltpu.make_async_copy(source, target, stores.at[n])
        for n, (source, target) in enumerate(
            [(leaf_pass, leaf_end), (row_out, row_end), (col_out, col_end), (root_out, root_end)]
        )
    ]
    copies[0].wait()
    copies[2].wait()
    copies[3].wait()
    for tree in range(2):
        grams[N_COL + N_ROW + tree, :, :RANK] = unpack(highest[tree])

    def spread_out(n, carry):
        for line in range(4):
            grams[line * 8 + n, :, :RANK] = unpack(row_table[line, n])
        for line in range(2):
            grams[N_COL + line * 8 + n, :, :RANK] = unpack(col_table[line, n])
        return carry

    lax.fori_loop(0, 8, spread_out, 0, unroll=2)
    to_lanes(grams, batch, ROOT_BATCH)
    factor(batch)
    copies[1].wait()
    results[0].start()
    from_lanes(batch, factors, (N_COL, N_ROW + 8))
    for tree, out in enumerate((row_out, col_out)):
        base = (N_COL + N_ROW + tree) * RANK
        even, odd = (factors[pl.ds(base + half, 32, stride=2), :][:, :RANK] for half in range(2))
        out[...] = jnp.concatenate([even, odd], 1)
    results[1].start()
    results[2].start()
    for copy in copies[4:]:
        copy.wait()

    def convert(first, entries, count):
        def step(n, carry):
            entries[n] = table_entry(factors[pl.ds(pl.multiple_of((first + n) * RANK, RANK), RANK), :][:, :RANK])
            return carry

        lax.fori_loop(0, count, step, 0, unroll=4)

    convert(0, root_left, N_COL)
    convert(N_COL, root_right, N_ROW)
    couple(
        ROOT_PAIRS,
        root_blocks,
        block_stage,
        root_left,
        root_right,
        lambda pair: lax.rem(root_rows[0, 0, pair], N_X) * 8 + lax.div(root_rows[0, 0, pair], N_X),
        lambda pair: lax.rem(root_cols[0, 0, pair], N_CORE) * 8 + lax.div(root_cols[0, 0, pair], N_CORE),
        root_out,
    )
    results[3].start()
    for result in results:
        result.wait()


def tiled(array, rows):
    return array.reshape(rows // 8, 8, 32, 128).transpose(0, 2, 1, 3).reshape(rows * 32, 128)


def untiled(array, rows):
    return array.reshape(rows // 8, 32, 8, 128).transpose(0, 2, 1, 3).reshape(1, rows, RANK * RANK)


def body(
    row_bases,
    col_bases,
    row_transfer,
    col_transfer,
    row_order,
    col_order,
    leaf_pattern,
    leaf_blocks,
    root_rows,
    root_cols,
    root_blocks,
):
    vmem, smem = pltpu.VMEM, pltpu.SMEM
    dma = pltpu.SemaphoreType.DMA
    hbm = pl.BlockSpec(memory_space=pltpu.HBM)
    shape = jax.ShapeDtypeStruct
    packed = (32, 128)
    scratch = [
        vmem((LEAF_PAIRS * 32, 128), F32),
        dma((4,)),
        smem((1, 1, LEAF_DEV), jnp.int32),
        smem((1, 1, LEAF_DEV), jnp.int32),
        smem((1, 2, LEAF_PAIRS), jnp.int32),
        vmem((2, 512, 128), F32),
        vmem((2, 1024, 128), F32),
        vmem((2048, 128), BF16),
        dma((8,)),
        vmem((2 * 32, RANK, 128), F32),
        vmem((2 * LEAF_DEV, RANK, 128), F32),
        vmem((2 * 16, RANK, 128), F32),
        vmem((RANK, RANK, 128), F32),
        vmem((2 * LEAF_DEV * RANK, 128), F32),
        vmem((LEAF_DEV, 2 * RANK, RANK), BF16),
        vmem((LEAF_DEV, 2 * RANK, RANK), BF16),
        vmem((256, 128), F32),
        vmem((2, *packed), F32),
        vmem((2, *packed), F32),
        vmem((2, RANK, RANK), F32),
        vmem((2, *packed), F32),
        vmem((2, 8, *packed), F32),
        dma((2, 8)),
        dma((2, 8)),
        dma((2, N_X)),
        dma((2, N_X)),
    ]
    for tree in range(2):
        for depth in STAGES[tree]:
            size = 1 << depth
            scratch += [
                vmem((depth, *packed), F32),
                vmem((depth, *packed), F32),
                vmem((size, *packed), F32),
                dma((size,)),
                dma((depth,)),
                dma((size,)),
                dma((size,)),
            ]
    parts = pl.pallas_call(
        kernel,
        out_shape=(
            shape((LEAF_PAIRS * 32, 128), F32),
            shape((2, *packed), F32),
            shape((N_X, N_Y, *packed), F32),
            shape((N_CORE, N_Z, *packed), F32),
        ),
        in_specs=[hbm] * 8,
        out_specs=(hbm,) * 4,
        scratch_shapes=scratch,
        compiler_params=pltpu.CompilerParams(
            collective_id=0, has_side_effects=True, vmem_limit_bytes=62 * 2**20
        ),
    )(
        row_order,
        col_order,
        leaf_pattern,
        tiled(row_bases, LEAF_DEV),
        tiled(col_bases, LEAF_DEV),
        tiled(row_transfer, 2 * LEAF_DEV),
        tiled(col_transfer, 2 * LEAF_DEV),
        tiled(leaf_blocks, LEAF_PAIRS),
    )
    leaf_out, root_out, row_out, col_out = pl.pallas_call(
        finish,
        out_shape=(
            shape((LEAF_PAIRS * 32, 128), F32),
            shape((ROOT_PAIRS * 32, 128), F32),
            shape(packed, F32),
            shape(packed, F32),
        ),
        in_specs=[hbm] * 7,
        out_specs=(hbm,) * 4,
        scratch_shapes=[
            vmem((LEAF_PAIRS * 32, 128), F32),
            vmem((2, *packed), F32),
            vmem((N_X, N_Y, *packed), F32),
            vmem((N_CORE, N_Z, *packed), F32),
            smem((1, 1, ROOT_PAIRS), jnp.int32),
            smem((1, 1, ROOT_PAIRS), jnp.int32),
            vmem((1024, 128), BF16),
            vmem((ROOT_PAIRS * 32, 128), F32),
            vmem(packed, F32),
            vmem(packed, F32),
            dma((7,)),
            dma((4,)),
            vmem((ROOT_BATCH, RANK, 128), F32),
            vmem((RANK, RANK, 128), F32),
            vmem((ROOT_BATCH * RANK, 128), F32),
            vmem((N_COL, 2 * RANK, RANK), BF16),
            vmem((N_ROW, 2 * RANK, RANK), BF16),
            vmem((256, 128), F32),
        ],
        compiler_params=pltpu.CompilerParams(vmem_limit_bytes=62 * 2**20),
    )(*parts, root_rows, root_cols, tiled(root_blocks, ROOT_PAIRS))
    return (
        untiled(leaf_out, LEAF_PAIRS),
        untiled(root_out, ROOT_PAIRS),
        row_out.reshape(1, 1, RANK * RANK),
        col_out.reshape(1, 1, RANK * RANK),
    )


def solution(mesh):
    return jax.shard_map(
        body,
        mesh=mesh,
        in_specs=(
            P("row", "col", None),
            P("col", "row", None),
            P("row", "col", None),
            P("col", "row", None),
            P("row", "col", None),
            P("col", "row", None),
            P("row", "col", None),
            P("row", "col", None),
            P("row", "col", None),
            P("row", "col", None),
            P("row", "col", None),
        ),
        out_specs=(
            P("row", "col", None),
            P("row", "col", None),
            P("row", "col", None),
            P("col", "row", None),
        ),
        check_vma=False,
    )
```

```python
import functools

import jax
import jax.numpy as jnp
from jax import lax
from jax.experimental import pallas as pl
from jax.experimental.pallas import tpu as pltpu
from jax.sharding import PartitionSpec as P

RANK = 64
LEAF_DEV = 16
LEAF_PAIRS = 64
ROOT_PAIRS = 32
N_ROW = 16
N_COL = 32
N_X = 4
N_Y = 8
N_Z = 8
N_CORE = 2
ROOT_BATCH = N_COL + N_ROW + 8
MESH = pl.DeviceIdType.MESH
F32 = jnp.float32
BF16 = jnp.bfloat16


def split(value):
    high = value.astype(BF16)
    return high, (value - high.astype(F32)).astype(BF16)


def contract(left, right, left_dim, right_dim):
    return lax.dot_general(
        left, right, (((left_dim,), (right_dim,)), ((), ())), preferred_element_type=F32
    )


def product_nn(left, right):
    left_high, left_low = split(left)
    right_high, right_low = split(right)
    both = contract(jnp.concatenate([left_high, left_low], 0), right_high, 1, 0)
    rows = left.shape[0]
    return both[:rows] + both[rows:] + contract(left_high, right_low, 1, 0)


def product_tn(left, right):
    return product_nn(left.T, right)


def sandwich(gram, transfer):
    return product_tn(transfer, product_nn(gram, transfer))


def pack(square):
    return jnp.concatenate([square[:32, :], square[32:, :]], 1)


def unpack(packed):
    return jnp.concatenate([packed[:, :RANK], packed[:, RANK:]], 0)


def level_of(place, depth):
    level = jnp.int32(depth)
    for k in range(depth - 1, 0, -1):
        level = jnp.where(lax.rem(place, 1 << k) == 1 << (k - 1), jnp.int32(k), level)
    return level


def span_of(place, depth):
    span = jnp.int32(1 << depth)
    for k in range(depth - 1, 0, -1):
        span = jnp.where(lax.rem(place, 1 << k) == 1 << (k - 1), jnp.int32(1 << k), span)
    return span


def fixed_level(place, depth):
    return depth if place == 0 else (place & -place).bit_length()


class Stage:
    def __init__(self, depth, place, taking_part, peer, refs):
        self.depth, self.size, self.place = depth, 1 << depth, place
        self.taking_part, self.peer = taking_part, peer
        (self.inner, self.terms, self.slots, self.inner_sent, self.inner_got, self.sent, self.got) = refs
        self.level = level_of(place, depth)
        self.span = span_of(place, depth)

    def inner_copy(self, target, level):
        return pltpu.make_async_remote_copy(
            self.own_inner,
            self.inner.at[level - 1],
            self.inner_sent.at[target],
            self.inner_got.at[level - 1],
            device_id=self.peer(target),
            device_id_type=MESH,
        )

    def each_inner_target(self, act):
        for target in range(self.size):
            same = lax.div(self.place, self.span) == lax.div(jnp.int32(target), self.span)
            wanted = (self.place != 0) & (self.place != target) & same
            if target != 0:
                wanted = wanted & (self.span < self.size)
            pl.when(self.taking_part & wanted)(functools.partial(act, target))

    def send_inner(self, own_inner):
        self.own_inner = own_inner
        self.each_inner_target(lambda target: self.inner_copy(target, self.level).start())

    def receive_inner(self):
        for level in range(1, self.depth + 1):
            half = 1 << (level - 1)
            if level < self.depth:
                mine = lax.rem(self.place, 2 * half) == half
                away = jnp.logical_not(mine)

                @pl.when(self.taking_part & mine)
                def _(level=level):
                    self.inner[level - 1] = self.own_inner[...]
            else:
                away = self.place == 0

            @pl.when(self.taking_part & away)
            def _(level=level):
                self.inner_copy(0, level).wait_recv()

    def make_terms(self, gram, transfer):
        path = transfer
        for level in range(1, self.depth + 1):
            self.terms[level - 1] = pack(sandwich(gram, path))
            if level < self.depth:
                path = product_nn(path, unpack(self.inner[level - 1]))

    def term_copy(self, target, sender):
        return pltpu.make_async_remote_copy(
            self.terms.at[fixed_level(target, self.depth) - 1],
            self.slots.at[sender],
            self.sent.at[target],
            self.got.at[sender],
            device_id=self.peer(target),
            device_id_type=MESH,
        )

    def each_target(self, act):
        for target in range(self.size):
            span = 1 << fixed_level(target, self.depth)
            wanted = (self.place != target) & (lax.div(self.place, span) == target // span)
            pl.when(self.taking_part & wanted)(functools.partial(act, target))

    def send_terms(self):
        self.each_target(lambda target: self.term_copy(target, self.place).start())

    def receive_terms(self, total_ref):
        @pl.when(self.taking_part)
        def _():
            total_ref[...] = self.terms[self.level - 1]

        for sender in range(self.size):
            same = lax.div(self.place, self.span) == lax.div(jnp.int32(sender), self.span)

            @pl.when(self.taking_part & (self.place != sender) & same)
            def _(sender=sender):
                self.term_copy(0, sender).wait_recv()
                total_ref[...] += self.slots[sender]

    def finish(self):
        self.each_inner_target(lambda target: self.inner_copy(target, self.level).wait_send())
        self.each_target(lambda target: self.term_copy(target, self.place).wait_send())


def to_lanes(gram_ref, batch_ref, count):
    flat = gram_ref.reshape(gram_ref.shape[0] * RANK, 128)

    def step(j, carry):
        rows = flat[pl.ds(j, count, stride=RANK), :]
        batch_ref[j, :, :count] = rows.T[:RANK, :]
        return carry

    lax.fori_loop(0, RANK, step, 0, unroll=32)


def factor(batch_ref):
    def diagonal(block):
        first, span = 8 * block, slice(8 * block, 8 * block + 8)
        columns = [batch_ref[first + c, span, :] for c in range(8)]
        inverses = []

        def step(c):
            inverse = lax.rsqrt(jnp.broadcast_to(columns[c][c : c + 1, :], (8, 128)))
            column = columns[c] * inverse
            batch_ref[first + c, span, :] = column
            inverses.append(inverse)
            for later in range(c + 1, 8):
                columns[later] = columns[later] - column * column[later : later + 1, :]

        return [functools.partial(step, c) for c in range(8)], inverses

    def below(block, other, inverses):
        first, span = 8 * block, slice(8 * other, 8 * other + 8)
        done = []
        for c in range(8):
            column = batch_ref[first + c, span, :]
            for k in range(c):
                column = column - done[k] * batch_ref[first + k, first + c : first + c + 1, :]
            column = column * inverses[c]
            batch_ref[first + c, span, :] = column
            done.append(column)

    def update(block, j, low, high):
        first, span = 8 * block, slice(8 * low, 8 * high)
        total = batch_ref[j, span, :]
        for c in range(8):
            total = total - batch_ref[first + c, span, :] * batch_ref[first + c, j : j + 1, :]
        batch_ref[j, span, :] = total

    steps, inverses = diagonal(0)
    for step in steps:
        step()
    for block in range(7):
        after = block + 1
        below(block, after, inverses)
        for j in range(8 * after, 8 * after + 8):
            update(block, j, after, after + 1)
        pieces = [functools.partial(below, block, other, inverses) for other in range(after + 1, 8)]
        if after < 7:
            pieces += [functools.partial(update, block, j, after + 1, 8) for j in range(8 * after, 8 * after + 8)]
        pieces += [functools.partial(update, block, j, j // 8, 8) for j in range(8 * after + 8, RANK)]
        steps, inverses = diagonal(after)
        for n, step in enumerate(steps):
            step()
            for piece in pieces[n * len(pieces) // 8 : (n + 1) * len(pieces) // 8]:
                piece()


def from_lanes(batch_ref, factor_ref, counts):
    place = lax.broadcasted_iota(jnp.int32, (RANK, 128), 0)
    first_group = lax.broadcasted_iota(jnp.int32, (RANK, 128), 1) < counts[0]
    halved = jnp.where(place < 32, 2 * place, 2 * place - 63)
    column = jnp.where(first_group, halved, place)

    def step(j, carry):
        plane = batch_ref.at[j]
        halves = jnp.concatenate([plane[pl.ds(0, 32, stride=2), :], plane[pl.ds(1, 32, stride=2), :]], 0)
        values = jnp.where(first_group, halves, plane[...])
        values = jnp.where(column >= j, values, 0.0).T
        moved = lax.div(j, 2) + 32 * lax.rem(j, 2)
        factor_ref[pl.ds(moved, counts[0], stride=RANK), :RANK] = values[: counts[0]]
        factor_ref[pl.ds(counts[0] * RANK + j, counts[1], stride=RANK), :RANK] = values[counts[0] : sum(counts)]
        return carry

    lax.fori_loop(0, RANK, step, 0, unroll=16)


def couple(count, blocks_ref, stage_ref, left_ref, right_ref, left_pick, right_pick, out_ref):
    first_half = lax.broadcasted_iota(jnp.int32, (1, 128), 1) < RANK

    def step(group, carry):
        base = pl.multiple_of(group * 256, 256)
        stage_ref[...] = blocks_ref[pl.ds(base, 256), :].astype(F32)
        for pair in range(8):
            packed = stage_ref[pl.ds(pair, 32, stride=8), :].astype(BF16)
            square = unpack(packed)
            left = left_ref[left_pick(group * 8 + pair)]
            right = right_ref[right_pick(group * 8 + pair)]
            both = contract(left, square, 1, 0)
            high, low = split(both[:RANK] + both[RANK:])
            out = contract(jnp.concatenate([high, low], 0), right, 1, 0)
            out = out[:RANK] + jnp.where(first_half, out[RANK:], 0.0)
            out = out + pltpu.roll(out, RANK, 1)
            out_ref[pl.ds(base + pair, 32, stride=8), :] = jnp.where(first_half, out[:32], out[32:])
        return carry

    lax.fori_loop(0, count // 8, step, 0, unroll=4)


def table_entry(value):
    return jnp.concatenate(split(value), 0)


def right_entry(value):
    high = value.astype(BF16).astype(F32)
    return jnp.concatenate([high, value - high], 0).T.astype(BF16)


STAGES = ((2, 3, 4), (4, 2, 3))


def kernel(
    row_order_hbm,
    col_order_hbm,
    leaf_pattern_hbm,
    row_bases_hbm,
    col_bases_hbm,
    row_transfer_hbm,
    col_transfer_hbm,
    leaf_blocks_hbm,
    leaf_hbm,
    highest_hbm,
    row_table,
    col_table,
    leaf_out,
    stores,
    row_order,
    col_order,
    leaf_pattern,
    bases,
    transfers,
    leaf_blocks,
    loads,
    natural,
    grams,
    nodes,
    batch,
    factors,
    leaf_left,
    leaf_right,
    block_stage,
    inner_own,
    highest,
    roots,
    root_own,
    root_line,
    line_sent,
    line_got,
    spread_sent,
    spread_got,
    *stage_refs,
):
    place_row = lax.axis_index("row")
    place_col = lax.axis_index("col")
    copies = [
        pltpu.make_async_copy(source, target, loads.at[n])
        for n, (source, target) in enumerate(
            [
                (row_transfer_hbm, transfers.at[0]),
                (col_transfer_hbm, transfers.at[1]),
                (row_bases_hbm, bases.at[0]),
                (col_bases_hbm, bases.at[1]),
                (row_order_hbm, row_order),
                (col_order_hbm, col_order),
                (leaf_blocks_hbm, leaf_blocks),
                (leaf_pattern_hbm, leaf_pattern),
            ]
        )
    ]
    for copy in copies:
        copy.start()
    leaf_store = pltpu.make_async_copy(leaf_out, leaf_hbm, stores.at[0])
    highest_store = pltpu.make_async_copy(highest, highest_hbm, stores.at[1])
    barrier = pltpu.get_barrier_semaphore()

    def greet(axis, size, place):
        def step(k, carry):
            pl.semaphore_signal(
                barrier, inc=1, device_id={axis: lax.rem(place + k, size)}, device_id_type=MESH
            )
            return carry

        lax.fori_loop(1, size, step, 0)

    greet("col", N_COL, place_col)
    greet("row", N_ROW, place_row)

    x_place = lax.rem(place_col, N_X)
    y_place = lax.div(place_col, N_X)
    always = place_row >= 0
    x_peer = lambda p: {"col": y_place * N_X + p}
    y_peer = lambda p: {"col": p * N_X}
    z_peer = lambda p: {"row": jnp.int32(p)}
    z_place = lax.div(place_row, N_CORE)
    core_place = lax.rem(place_row, N_CORE)
    line_places = (y_place, z_place)

    def line_copy(tree, k, slot):
        place = lax.rem(line_places[tree] + k, 8)
        peer = {"col": place * N_X + x_place} if tree == 0 else {"row": place * N_CORE + core_place}
        return pltpu.make_async_remote_copy(
            root_own.at[tree],
            root_line.at[tree, slot],
            line_sent.at[tree, k],
            line_got.at[tree, slot],
            device_id=peer,
            device_id_type=MESH,
        )

    spreads = ((row_table, N_X, x_place), (col_table, N_CORE, core_place))

    def spread_copy(tree, k, slot):
        table, size, place = spreads[tree]
        to = lax.rem(place + k, size)
        peer = {"col": y_place * N_X + to} if tree == 0 else {"row": z_place * N_CORE + to}
        return pltpu.make_async_remote_copy(
            root_line.at[tree],
            table.at[slot],
            spread_sent.at[tree, k],
            spread_got.at[tree, slot],
            device_id=peer,
            device_id_type=MESH,
        )

    spread_copies = [[spread_copy(tree, k, spreads[tree][2]) for k in range(1, spreads[tree][1])] for tree in range(2)]
    keep_copies = [
        pltpu.make_async_copy(root_line.at[tree], spreads[tree][0].at[spreads[tree][2]], stores.at[2 + tree])
        for tree in range(2)
    ]
    layout = (
        (
            (x_place, always, x_peer),
            (y_place, x_place == 0, y_peer),
            (place_row, place_col == 0, z_peer),
        ),
        (
            (place_row, always, z_peer),
            (x_place, place_row == 0, x_peer),
            (y_place, (place_row == 0) & (x_place == 0), y_peer),
        ),
    )
    stages = []
    for tree in range(2):
        stages.append([])
        for n in range(3):
            at = 7 * (3 * tree + n)
            stages[tree].append(Stage(STAGES[tree][n], *layout[tree][n], stage_refs[at : at + 7]))

    for copy in copies[:2]:
        copy.wait()
    for tree in range(2):

        def lay_out(m, carry, tree=tree):
            rows = transfers[tree, pl.ds(lax.div(m, 8) * 256 + lax.rem(m, 8), 32, stride=8), :]
            place = natural.at[tree * 32 + m]
            place[pl.ds(0, 32, stride=2), :] = rows
            place[pl.ds(1, 32, stride=2), :] = pltpu.roll(rows, RANK, 1)
            return carry

        lax.fori_loop(0, 32, lay_out, 0, unroll=16)

    def transfer_of(tree, m):
        return natural[tree * 32 + m][:, :RANK]

    for tree in range(2):
        inner_own[tree] = pack(transfer_of(tree, 31))
    pl.semaphore_wait(barrier, N_COL + N_ROW - 2)
    for tree in range(2):
        for n in range(3):
            stages[tree][n].send_inner(inner_own.at[tree])

    for copy in copies[2:6]:
        copy.wait()

    def leaf_gram(leaf, carry):
        for tree in range(2):
            rows = bases[tree, pl.ds(lax.div(leaf, 8) * 256 + lax.rem(leaf, 8), 32, stride=8), :]
            basis = unpack(rows)
            grams[tree * LEAF_DEV + leaf, :, :RANK] = product_tn(basis, basis)
        return carry

    lax.fori_loop(0, LEAF_DEV, leaf_gram, 0, unroll=16)

    orders = (row_order, col_order)

    def first_level(q, carry):
        for tree in range(2):
            total = None
            for child in range(2):
                leaf = orders[tree][0, 0, 2 * q + child]
                term = sandwich(grams[tree * LEAF_DEV + leaf][:, :RANK], transfer_of(tree, leaf))
                total = term if total is None else total + term
            nodes[tree * 16 + q, :, :RANK] = total
        return carry

    lax.fori_loop(0, 8, first_level, 0, unroll=8)
    source, target, offset, count = 0, 8, 16, 8
    while count > 1:
        for tree in range(2):
            for q in range(count // 2):
                total = None
                for child in range(2):
                    node = 2 * q + child
                    term = sandwich(
                        nodes[tree * 16 + source + node][:, :RANK], transfer_of(tree, offset + node)
                    )
                    total = term if total is None else total + term
                if count > 2:
                    nodes[tree * 16 + target + q, :, :RANK] = total
                else:
                    roots[tree] = total
        offset += count
        source, target, count = target, target + count // 2, count // 2

    for tree in range(2):
        stage = stages[tree][0]
        stage.receive_inner()
        stage.make_terms(roots[tree], transfer_of(tree, 30))
        stage.send_terms()

    for tree in range(2):
        root_own[tree] = pack(roots[tree])
        root_line[tree, line_places[tree]] = root_own[tree]
    for tree in range(2):
        for k in range(1, 8):
            line_copy(tree, k, line_places[tree]).start()

    to_lanes(grams, batch, 2 * LEAF_DEV)
    factor(batch)
    from_lanes(batch, factors, (LEAF_DEV, LEAF_DEV))
    for tree in range(2):
        for k in range(1, 8):
            line_copy(tree, k, lax.rem(line_places[tree] + 8 - k, 8)).wait_recv()
        for copy in keep_copies[tree : tree + 1] + spread_copies[tree]:
            copy.start()
    for leaf in range(LEAF_DEV):
        leaf_left[leaf] = table_entry(factors[leaf * RANK : (leaf + 1) * RANK, :RANK])
        leaf_right[leaf] = right_entry(factors[(LEAF_DEV + leaf) * RANK : (LEAF_DEV + leaf + 1) * RANK, :RANK])

    def climb(n):
        for tree in range(2):
            stages[tree][n - 1].receive_terms(highest.at[tree])
            stage = stages[tree][n]
            stage.receive_inner()

            @pl.when(stage.taking_part)
            def _(stage=stage, tree=tree, n=n):
                exit_transfer = unpack(stages[tree][n - 1].inner[stages[tree][n - 1].depth - 1])
                stage.make_terms(unpack(highest[tree]), exit_transfer)

            stage.send_terms()

    climb(1)
    for copy in copies[6:8]:
        copy.wait()
    couple(
        LEAF_PAIRS,
        leaf_blocks,
        block_stage,
        leaf_left,
        leaf_right,
        lambda pair: leaf_pattern[0, 0, pair],
        lambda pair: leaf_pattern[0, 1, pair],
        leaf_out,
    )
    leaf_store.start()
    climb(2)

    for tree in range(2):
        stages[tree][2].receive_terms(highest.at[tree])
    highest_store.start()
    for tree in range(2):
        for k in range(1, spreads[tree][1]):
            spread_copy(tree, k, lax.rem(spreads[tree][2] + spreads[tree][1] - k, spreads[tree][1])).wait_recv()
    for tree in range(2):
        for n in range(3):
            stages[tree][n].finish()
    for tree in range(2):
        for k in range(1, 8):
            line_copy(tree, k, line_places[tree]).wait_send()
        for copy in spread_copies[tree]:
            copy.wait_send()
    for store in (leaf_store, highest_store, *keep_copies):
        store.wait()


def finish(
    leaf_hbm,
    highest_hbm,
    row_table_hbm,
    col_table_hbm,
    root_rows_hbm,
    root_cols_hbm,
    root_blocks_hbm,
    leaf_end,
    root_end,
    row_end,
    col_end,
    leaf_pass,
    highest,
    row_table,
    col_table,
    root_rows,
    root_cols,
    root_blocks,
    root_out,
    row_out,
    col_out,
    loads,
    stores,
    grams,
    batch,
    factors,
    root_left,
    root_right,
    block_stage,
):
    copies = [
        pltpu.make_async_copy(source, target, loads.at[n])
        for n, (source, target) in enumerate(
            [
                (highest_hbm, highest),
                (leaf_hbm, leaf_pass),
                (row_table_hbm, row_table),
                (col_table_hbm, col_table),
                (root_rows_hbm, root_rows),
                (root_cols_hbm, root_cols),
                (root_blocks_hbm, root_blocks),
            ]
        )
    ]
    for copy in copies:
        copy.start()
    results = [
        pltpu.make_async_copy(source, target, stores.at[n])
        for n, (source, target) in enumerate(
            [(leaf_pass, leaf_end), (row_out, row_end), (col_out, col_end), (root_out, root_end)]
        )
    ]
    copies[0].wait()
    copies[2].wait()
    copies[3].wait()
    for tree in range(2):
        grams[N_COL + N_ROW + tree, :, :RANK] = unpack(highest[tree])

    def spread_out(n, carry):
        for line in range(4):
            grams[line * 8 + n, :, :RANK] = unpack(row_table[line, n])
        for line in range(2):
            grams[N_COL + line * 8 + n, :, :RANK] = unpack(col_table[line, n])
        return carry

    lax.fori_loop(0, 8, spread_out, 0, unroll=8)
    to_lanes(grams, batch, ROOT_BATCH)
    factor(batch)
    copies[1].wait()
    results[0].start()
    from_lanes(batch, factors, (N_COL, N_ROW + 8))
    for tree, out in enumerate((row_out, col_out)):
        base = (N_COL + N_ROW + tree) * RANK
        even, odd = (factors[pl.ds(base + half, 32, stride=2), :][:, :RANK] for half in range(2))
        out[...] = jnp.concatenate([even, odd], 1)
    results[1].start()
    results[2].start()
    for copy in copies[4:]:
        copy.wait()

    def convert(first, entries, count, entry):
        def step(n, carry):
            entries[n] = entry(factors[pl.ds(pl.multiple_of((first + n) * RANK, RANK), RANK), :][:, :RANK])
            return carry

        lax.fori_loop(0, count, step, 0, unroll=16)

    convert(0, root_left, N_COL, table_entry)
    convert(N_COL, root_right, N_ROW, right_entry)
    couple(
        ROOT_PAIRS,
        root_blocks,
        block_stage,
        root_left,
        root_right,
        lambda pair: lax.rem(root_rows[0, 0, pair], N_X) * 8 + lax.div(root_rows[0, 0, pair], N_X),
        lambda pair: lax.rem(root_cols[0, 0, pair], N_CORE) * 8 + lax.div(root_cols[0, 0, pair], N_CORE),
        root_out,
    )
    results[3].start()
    for result in results:
        result.wait()


def tiled(array, rows):
    return array.reshape(rows // 8, 8, 32, 128).transpose(0, 2, 1, 3).reshape(rows * 32, 128)


def untiled(array, rows):
    return array.reshape(rows // 8, 32, 8, 128).transpose(0, 2, 1, 3).reshape(1, rows, RANK * RANK)


def body(
    row_bases,
    col_bases,
    row_transfer,
    col_transfer,
    row_order,
    col_order,
    leaf_pattern,
    leaf_blocks,
    root_rows,
    root_cols,
    root_blocks,
):
    vmem, smem = pltpu.VMEM, pltpu.SMEM
    dma = pltpu.SemaphoreType.DMA
    hbm = pl.BlockSpec(memory_space=pltpu.HBM)
    shape = jax.ShapeDtypeStruct
    packed = (32, 128)
    scratch = [
        vmem((LEAF_PAIRS * 32, 128), F32),
        dma((4,)),
        smem((1, 1, LEAF_DEV), jnp.int32),
        smem((1, 1, LEAF_DEV), jnp.int32),
        smem((1, 2, LEAF_PAIRS), jnp.int32),
        vmem((2, 512, 128), F32),
        vmem((2, 1024, 128), F32),
        vmem((2048, 128), BF16),
        dma((8,)),
        vmem((2 * 32, RANK, 128), F32),
        vmem((2 * LEAF_DEV, RANK, 128), F32),
        vmem((2 * 16, RANK, 128), F32),
        vmem((RANK, RANK, 128), F32),
        vmem((2 * LEAF_DEV * RANK, 128), F32),
        vmem((LEAF_DEV, 2 * RANK, RANK), BF16),
        vmem((LEAF_DEV, RANK, 2 * RANK), BF16),
        vmem((256, 128), F32),
        vmem((2, *packed), F32),
        vmem((2, *packed), F32),
        vmem((2, RANK, RANK), F32),
        vmem((2, *packed), F32),
        vmem((2, 8, *packed), F32),
        dma((2, 8)),
        dma((2, 8)),
        dma((2, N_X)),
        dma((2, N_X)),
    ]
    for tree in range(2):
        for depth in STAGES[tree]:
            size = 1 << depth
            scratch += [
                vmem((depth, *packed), F32),
                vmem((depth, *packed), F32),
                vmem((size, *packed), F32),
                dma((size,)),
                dma((depth,)),
                dma((size,)),
                dma((size,)),
            ]
    parts = pl.pallas_call(
        kernel,
        out_shape=(
            shape((LEAF_PAIRS * 32, 128), F32),
            shape((2, *packed), F32),
            shape((N_X, N_Y, *packed), F32),
            shape((N_CORE, N_Z, *packed), F32),
        ),
        in_specs=[hbm] * 8,
        out_specs=(hbm,) * 4,
        scratch_shapes=scratch,
        compiler_params=pltpu.CompilerParams(
            collective_id=0, has_side_effects=True, vmem_limit_bytes=62 * 2**20
        ),
    )(
        row_order,
        col_order,
        leaf_pattern,
        tiled(row_bases, LEAF_DEV),
        tiled(col_bases, LEAF_DEV),
        tiled(row_transfer, 2 * LEAF_DEV),
        tiled(col_transfer, 2 * LEAF_DEV),
        tiled(leaf_blocks, LEAF_PAIRS),
    )
    leaf_out, root_out, row_out, col_out = pl.pallas_call(
        finish,
        out_shape=(
            shape((LEAF_PAIRS * 32, 128), F32),
            shape((ROOT_PAIRS * 32, 128), F32),
            shape(packed, F32),
            shape(packed, F32),
        ),
        in_specs=[hbm] * 7,
        out_specs=(hbm,) * 4,
        scratch_shapes=[
            vmem((LEAF_PAIRS * 32, 128), F32),
            vmem((2, *packed), F32),
            vmem((N_X, N_Y, *packed), F32),
            vmem((N_CORE, N_Z, *packed), F32),
            smem((1, 1, ROOT_PAIRS), jnp.int32),
            smem((1, 1, ROOT_PAIRS), jnp.int32),
            vmem((1024, 128), BF16),
            vmem((ROOT_PAIRS * 32, 128), F32),
            vmem(packed, F32),
            vmem(packed, F32),
            dma((7,)),
            dma((4,)),
            vmem((ROOT_BATCH, RANK, 128), F32),
            vmem((RANK, RANK, 128), F32),
            vmem((ROOT_BATCH * RANK, 128), F32),
            vmem((N_COL, 2 * RANK, RANK), BF16),
            vmem((N_ROW, RANK, 2 * RANK), BF16),
            vmem((256, 128), F32),
        ],
        compiler_params=pltpu.CompilerParams(vmem_limit_bytes=62 * 2**20),
    )(*parts, root_rows, root_cols, tiled(root_blocks, ROOT_PAIRS))
    return (
        untiled(leaf_out, LEAF_PAIRS),
        untiled(root_out, ROOT_PAIRS),
        row_out.reshape(1, 1, RANK * RANK),
        col_out.reshape(1, 1, RANK * RANK),
    )


def solution(mesh):
    return jax.shard_map(
        body,
        mesh=mesh,
        in_specs=(
            P("row", "col", None),
            P("col", "row", None),
            P("row", "col", None),
            P("col", "row", None),
            P("row", "col", None),
            P("col", "row", None),
            P("row", "col", None),
            P("row", "col", None),
            P("row", "col", None),
            P("row", "col", None),
            P("row", "col", None),
        ),
        out_specs=(
            P("row", "col", None),
            P("row", "col", None),
            P("row", "col", None),
            P("col", "row", None),
        ),
        check_vma=False,
    )
```

```python
import functools

import jax
import jax.numpy as jnp
from jax import lax
from jax.experimental import pallas as pl
from jax.experimental.pallas import tpu as pltpu
from jax.sharding import PartitionSpec as P

RANK = 64
LEAF_DEV = 16
LEAF_PAIRS = 64
ROOT_PAIRS = 32
N_ROW = 16
N_COL = 32
N_X = 4
N_Y = 8
N_Z = 8
N_CORE = 2
ROOT_BATCH = N_COL + N_ROW + 8
MESH = pl.DeviceIdType.MESH
F32 = jnp.float32
BF16 = jnp.bfloat16


def split(value):
    high = value.astype(BF16)
    return high, (value - high.astype(F32)).astype(BF16)


def contract(left, right, left_dim, right_dim):
    return lax.dot_general(
        left, right, (((left_dim,), (right_dim,)), ((), ())), preferred_element_type=F32
    )


def product_nn(left, right):
    left_high, left_low = split(left)
    right_high, right_low = split(right)
    both = contract(jnp.concatenate([left_high, left_low], 0), right_high, 1, 0)
    rows = left.shape[0]
    return both[:rows] + both[rows:] + contract(left_high, right_low, 1, 0)


def product_tn(left, right):
    return product_nn(left.T, right)


def sandwich(gram, transfer):
    return product_tn(transfer, product_nn(gram, transfer))


def pack(square):
    return jnp.concatenate([square[:32, :], square[32:, :]], 1)


def unpack(packed):
    return jnp.concatenate([packed[:, :RANK], packed[:, RANK:]], 0)


def level_of(place, depth):
    level = jnp.int32(depth)
    for k in range(depth - 1, 0, -1):
        level = jnp.where(lax.rem(place, 1 << k) == 1 << (k - 1), jnp.int32(k), level)
    return level


def span_of(place, depth):
    span = jnp.int32(1 << depth)
    for k in range(depth - 1, 0, -1):
        span = jnp.where(lax.rem(place, 1 << k) == 1 << (k - 1), jnp.int32(1 << k), span)
    return span


def fixed_level(place, depth):
    return depth if place == 0 else (place & -place).bit_length()


class Stage:
    def __init__(self, depth, place, taking_part, peer, refs):
        self.depth, self.size, self.place = depth, 1 << depth, place
        self.taking_part, self.peer = taking_part, peer
        (self.inner, self.paths, self.terms, self.slots, self.inner_sent, self.inner_got, self.sent, self.got) = refs
        self.level = level_of(place, depth)
        self.span = span_of(place, depth)

    def inner_copy(self, target, level):
        return pltpu.make_async_remote_copy(
            self.own_inner,
            self.inner.at[level - 1],
            self.inner_sent.at[target],
            self.inner_got.at[level - 1],
            device_id=self.peer(target),
            device_id_type=MESH,
        )

    def each_inner_target(self, act):
        for target in range(self.size):
            same = lax.div(self.place, self.span) == lax.div(jnp.int32(target), self.span)
            wanted = (self.place != 0) & (self.place != target) & same
            if target != 0:
                wanted = wanted & (self.span < self.size)
            pl.when(self.taking_part & wanted)(functools.partial(act, target))

    def send_inner(self, own_inner):
        self.own_inner = own_inner
        self.each_inner_target(lambda target: self.inner_copy(target, self.level).start())

    def receive_inner(self):
        for level in range(1, self.depth + 1):
            half = 1 << (level - 1)
            if level < self.depth:
                mine = lax.rem(self.place, 2 * half) == half
                away = jnp.logical_not(mine)

                @pl.when(self.taking_part & mine)
                def _(level=level):
                    self.inner[level - 1] = self.own_inner[...]
            else:
                away = self.place == 0

            @pl.when(self.taking_part & away)
            def _(level=level):
                self.inner_copy(0, level).wait_recv()

    def make_paths(self, transfer):
        path = transfer
        for level in range(1, self.depth + 1):
            self.paths[level - 1] = path
            if level < self.depth:
                path = product_nn(path, unpack(self.inner[level - 1]))

    def make_terms(self, gram):
        for level in range(1, self.depth + 1):
            self.terms[level - 1] = pack(sandwich(gram, self.paths[level - 1]))

    def term_copy(self, target, sender):
        return pltpu.make_async_remote_copy(
            self.terms.at[fixed_level(target, self.depth) - 1],
            self.slots.at[sender],
            self.sent.at[target],
            self.got.at[sender],
            device_id=self.peer(target),
            device_id_type=MESH,
        )

    def each_target(self, act):
        for target in range(self.size):
            span = 1 << fixed_level(target, self.depth)
            wanted = (self.place != target) & (lax.div(self.place, span) == target // span)
            pl.when(self.taking_part & wanted)(functools.partial(act, target))

    def send_terms(self):
        self.each_target(lambda target: self.term_copy(target, self.place).start())

    def receive_terms(self, total_ref):
        @pl.when(self.taking_part)
        def _():
            total_ref[...] = self.terms[self.level - 1]

        for sender in range(self.size):
            same = lax.div(self.place, self.span) == lax.div(jnp.int32(sender), self.span)

            @pl.when(self.taking_part & (self.place != sender) & same)
            def _(sender=sender):
                self.term_copy(0, sender).wait_recv()
                total_ref[...] += self.slots[sender]

    def finish(self):
        self.each_inner_target(lambda target: self.inner_copy(target, self.level).wait_send())
        self.each_target(lambda target: self.term_copy(target, self.place).wait_send())


def to_lanes(gram_ref, batch_ref, count):
    flat = gram_ref.reshape(gram_ref.shape[0] * RANK, 128)

    def step(j, carry):
        rows = flat[pl.ds(j, count, stride=RANK), :]
        batch_ref[j, :, :count] = rows.T[:RANK, :]
        return carry

    lax.fori_loop(0, RANK, step, 0, unroll=32)


def factor(batch_ref):
    def diagonal(block):
        first, span = 8 * block, slice(8 * block, 8 * block + 8)
        columns = [batch_ref[first + c, span, :] for c in range(8)]
        inverses = []

        def step(c):
            inverse = lax.rsqrt(jnp.broadcast_to(columns[c][c : c + 1, :], (8, 128)))
            column = columns[c] * inverse
            batch_ref[first + c, span, :] = column
            inverses.append(inverse)
            for later in range(c + 1, 8):
                columns[later] = columns[later] - column * column[later : later + 1, :]

        return [functools.partial(step, c) for c in range(8)], inverses

    def below(block, other, inverses):
        first, span = 8 * block, slice(8 * other, 8 * other + 8)
        done = []
        for c in range(8):
            column = batch_ref[first + c, span, :]
            for k in range(c):
                column = column - done[k] * batch_ref[first + k, first + c : first + c + 1, :]
            column = column * inverses[c]
            batch_ref[first + c, span, :] = column
            done.append(column)

    def update(block, j, low, high):
        first, span = 8 * block, slice(8 * low, 8 * high)
        total = batch_ref[j, span, :]
        for c in range(8):
            total = total - batch_ref[first + c, span, :] * batch_ref[first + c, j : j + 1, :]
        batch_ref[j, span, :] = total

    steps, inverses = diagonal(0)
    for step in steps:
        step()
    for block in range(7):
        after = block + 1
        below(block, after, inverses)
        for j in range(8 * after, 8 * after + 8):
            update(block, j, after, after + 1)
        pieces = [functools.partial(below, block, other, inverses) for other in range(after + 1, 8)]
        if after < 7:
            pieces += [functools.partial(update, block, j, after + 1, 8) for j in range(8 * after, 8 * after + 8)]
        pieces += [functools.partial(update, block, j, j // 8, 8) for j in range(8 * after + 8, RANK)]
        steps, inverses = diagonal(after)
        for n, step in enumerate(steps):
            step()
            for piece in pieces[n * len(pieces) // 8 : (n + 1) * len(pieces) // 8]:
                piece()


def from_lanes(batch_ref, factor_ref, counts):
    place = lax.broadcasted_iota(jnp.int32, (RANK, 128), 0)
    first_group = lax.broadcasted_iota(jnp.int32, (RANK, 128), 1) < counts[0]
    halved = jnp.where(place < 32, 2 * place, 2 * place - 63)
    column = jnp.where(first_group, halved, place)

    def step(j, carry):
        plane = batch_ref.at[j]
        halves = jnp.concatenate([plane[pl.ds(0, 32, stride=2), :], plane[pl.ds(1, 32, stride=2), :]], 0)
        values = jnp.where(first_group, halves, plane[...])
        values = jnp.where(column >= j, values, 0.0).T
        moved = lax.div(j, 2) + 32 * lax.rem(j, 2)
        factor_ref[pl.ds(moved, counts[0], stride=RANK), :RANK] = values[: counts[0]]
        factor_ref[pl.ds(counts[0] * RANK + j, counts[1], stride=RANK), :RANK] = values[counts[0] : sum(counts)]
        return carry

    lax.fori_loop(0, RANK, step, 0, unroll=16)


def couple(count, blocks_ref, stage_ref, left_ref, right_ref, left_pick, right_pick, out_ref):
    first_half = lax.broadcasted_iota(jnp.int32, (1, 128), 1) < RANK

    def step(group, carry):
        base = pl.multiple_of(group * 256, 256)
        stage_ref[...] = blocks_ref[pl.ds(base, 256), :].astype(F32)
        for pair in range(8):
            packed = stage_ref[pl.ds(pair, 32, stride=8), :].astype(BF16)
            square = unpack(packed)
            left = left_ref[left_pick(group * 8 + pair)]
            right = right_ref[right_pick(group * 8 + pair)]
            both = contract(left, square, 1, 0)
            high, low = split(both[:RANK] + both[RANK:])
            out = contract(jnp.concatenate([high, low], 0), right, 1, 0)
            out = out[:RANK] + jnp.where(first_half, out[RANK:], 0.0)
            out = out + pltpu.roll(out, RANK, 1)
            out_ref[pl.ds(base + pair, 32, stride=8), :] = jnp.where(first_half, out[:32], out[32:])
        return carry

    lax.fori_loop(0, count // 8, step, 0, unroll=4)


def table_entry(value):
    return jnp.concatenate(split(value), 0)


def right_entry(value):
    high = value.astype(BF16).astype(F32)
    return jnp.concatenate([high, value - high], 0).T.astype(BF16)


STAGES = ((2, 3, 4), (4, 2, 3))


def kernel(
    row_order_hbm,
    col_order_hbm,
    leaf_pattern_hbm,
    row_bases_hbm,
    col_bases_hbm,
    row_transfer_hbm,
    col_transfer_hbm,
    leaf_blocks_hbm,
    leaf_hbm,
    highest_hbm,
    row_table,
    col_table,
    leaf_out,
    stores,
    row_order,
    col_order,
    leaf_pattern,
    bases,
    transfers,
    leaf_blocks,
    loads,
    natural,
    grams,
    nodes,
    batch,
    factors,
    leaf_left,
    leaf_right,
    block_stage,
    inner_own,
    highest,
    roots,
    root_own,
    root_line,
    line_sent,
    line_got,
    spread_sent,
    spread_got,
    *stage_refs,
):
    place_row = lax.axis_index("row")
    place_col = lax.axis_index("col")
    copies = [
        pltpu.make_async_copy(source, target, loads.at[n])
        for n, (source, target) in enumerate(
            [
                (row_transfer_hbm, transfers.at[0]),
                (col_transfer_hbm, transfers.at[1]),
                (row_bases_hbm, bases.at[0]),
                (col_bases_hbm, bases.at[1]),
                (row_order_hbm, row_order),
                (col_order_hbm, col_order),
                (leaf_blocks_hbm, leaf_blocks),
                (leaf_pattern_hbm, leaf_pattern),
            ]
        )
    ]
    for copy in copies:
        copy.start()
    leaf_store = pltpu.make_async_copy(leaf_out, leaf_hbm, stores.at[0])
    highest_store = pltpu.make_async_copy(highest, highest_hbm, stores.at[1])
    barrier = pltpu.get_barrier_semaphore()

    def greet(axis, size, place):
        def step(k, carry):
            pl.semaphore_signal(
                barrier, inc=1, device_id={axis: lax.rem(place + k, size)}, device_id_type=MESH
            )
            return carry

        lax.fori_loop(1, size, step, 0)

    greet("col", N_COL, place_col)
    greet("row", N_ROW, place_row)

    x_place = lax.rem(place_col, N_X)
    y_place = lax.div(place_col, N_X)
    always = place_row >= 0
    x_peer = lambda p: {"col": y_place * N_X + p}
    y_peer = lambda p: {"col": p * N_X}
    z_peer = lambda p: {"row": jnp.int32(p)}
    z_place = lax.div(place_row, N_CORE)
    core_place = lax.rem(place_row, N_CORE)
    line_places = (y_place, z_place)

    def line_copy(tree, k, slot):
        place = lax.rem(line_places[tree] + k, 8)
        peer = {"col": place * N_X + x_place} if tree == 0 else {"row": place * N_CORE + core_place}
        return pltpu.make_async_remote_copy(
            root_own.at[tree],
            root_line.at[tree, slot],
            line_sent.at[tree, k],
            line_got.at[tree, slot],
            device_id=peer,
            device_id_type=MESH,
        )

    spreads = ((row_table, N_X, x_place), (col_table, N_CORE, core_place))

    def spread_copy(tree, k, slot):
        table, size, place = spreads[tree]
        to = lax.rem(place + k, size)
        peer = {"col": y_place * N_X + to} if tree == 0 else {"row": z_place * N_CORE + to}
        return pltpu.make_async_remote_copy(
            root_line.at[tree],
            table.at[slot],
            spread_sent.at[tree, k],
            spread_got.at[tree, slot],
            device_id=peer,
            device_id_type=MESH,
        )

    spread_copies = [[spread_copy(tree, k, spreads[tree][2]) for k in range(1, spreads[tree][1])] for tree in range(2)]
    keep_copies = [
        pltpu.make_async_copy(root_line.at[tree], spreads[tree][0].at[spreads[tree][2]], stores.at[2 + tree])
        for tree in range(2)
    ]
    layout = (
        (
            (x_place, always, x_peer),
            (y_place, x_place == 0, y_peer),
            (place_row, place_col == 0, z_peer),
        ),
        (
            (place_row, always, z_peer),
            (x_place, place_row == 0, x_peer),
            (y_place, (place_row == 0) & (x_place == 0), y_peer),
        ),
    )
    stages = []
    for tree in range(2):
        stages.append([])
        for n in range(3):
            at = 8 * (3 * tree + n)
            stages[tree].append(Stage(STAGES[tree][n], *layout[tree][n], stage_refs[at : at + 8]))

    for copy in copies[:2]:
        copy.wait()
    for tree in range(2):

        def lay_out(m, carry, tree=tree):
            rows = transfers[tree, pl.ds(lax.div(m, 8) * 256 + lax.rem(m, 8), 32, stride=8), :]
            place = natural.at[tree * 32 + m]
            place[pl.ds(0, 32, stride=2), :] = rows
            place[pl.ds(1, 32, stride=2), :] = pltpu.roll(rows, RANK, 1)
            return carry

        lax.fori_loop(0, 32, lay_out, 0, unroll=16)

    def transfer_of(tree, m):
        return natural[tree * 32 + m][:, :RANK]

    for tree in range(2):
        inner_own[tree] = pack(transfer_of(tree, 31))
    pl.semaphore_wait(barrier, N_COL + N_ROW - 2)
    for tree in range(2):
        for n in range(3):
            stages[tree][n].send_inner(inner_own.at[tree])

    for copy in copies[2:6]:
        copy.wait()

    def leaf_gram(leaf, carry):
        for tree in range(2):
            rows = bases[tree, pl.ds(lax.div(leaf, 8) * 256 + lax.rem(leaf, 8), 32, stride=8), :]
            basis = unpack(rows)
            grams[tree * LEAF_DEV + leaf, :, :RANK] = product_tn(basis, basis)
        return carry

    lax.fori_loop(0, LEAF_DEV, leaf_gram, 0, unroll=16)

    orders = (row_order, col_order)

    def first_level(q, carry):
        for tree in range(2):
            total = None
            for child in range(2):
                leaf = orders[tree][0, 0, 2 * q + child]
                term = sandwich(grams[tree * LEAF_DEV + leaf][:, :RANK], transfer_of(tree, leaf))
                total = term if total is None else total + term
            nodes[tree * 16 + q, :, :RANK] = total
        return carry

    lax.fori_loop(0, 8, first_level, 0, unroll=8)
    for tree in range(2):
        stages[tree][0].receive_inner()
    for tree in range(2):
        stages[tree][0].make_paths(transfer_of(tree, 30))
    source, target, offset, count = 0, 8, 16, 8
    while count > 1:
        for tree in range(2):
            for q in range(count // 2):
                total = None
                for child in range(2):
                    node = 2 * q + child
                    term = sandwich(
                        nodes[tree * 16 + source + node][:, :RANK], transfer_of(tree, offset + node)
                    )
                    total = term if total is None else total + term
                if count > 2:
                    nodes[tree * 16 + target + q, :, :RANK] = total
                else:
                    roots[tree] = total
        offset += count
        source, target, count = target, target + count // 2, count // 2

    for tree in range(2):
        stage = stages[tree][0]
        stage.make_terms(roots[tree])
        stage.send_terms()

    for tree in range(2):
        root_own[tree] = pack(roots[tree])
        root_line[tree, line_places[tree]] = root_own[tree]
    for tree in range(2):
        for k in range(1, 8):
            line_copy(tree, k, line_places[tree]).start()

    to_lanes(grams, batch, 2 * LEAF_DEV)
    factor(batch)
    from_lanes(batch, factors, (LEAF_DEV, LEAF_DEV))
    for n in range(1, 3):
        for tree in range(2):
            stage, before = stages[tree][n], stages[tree][n - 1]
            stage.receive_inner()

            @pl.when(stage.taking_part)
            def _(stage=stage, before=before):
                stage.make_paths(unpack(before.inner[before.depth - 1]))

    for tree in range(2):
        for k in range(1, 8):
            line_copy(tree, k, lax.rem(line_places[tree] + 8 - k, 8)).wait_recv()
        for copy in keep_copies[tree : tree + 1] + spread_copies[tree]:
            copy.start()
    for leaf in range(LEAF_DEV):
        leaf_left[leaf] = table_entry(factors[leaf * RANK : (leaf + 1) * RANK, :RANK])
        leaf_right[leaf] = right_entry(factors[(LEAF_DEV + leaf) * RANK : (LEAF_DEV + leaf + 1) * RANK, :RANK])

    def climb(n):
        for tree in range(2):
            stages[tree][n - 1].receive_terms(highest.at[tree])
            stage = stages[tree][n]

            @pl.when(stage.taking_part)
            def _(stage=stage, tree=tree):
                stage.make_terms(unpack(highest[tree]))

            stage.send_terms()

    climb(1)
    for copy in copies[6:8]:
        copy.wait()
    couple(
        LEAF_PAIRS,
        leaf_blocks,
        block_stage,
        leaf_left,
        leaf_right,
        lambda pair: leaf_pattern[0, 0, pair],
        lambda pair: leaf_pattern[0, 1, pair],
        leaf_out,
    )
    leaf_store.start()
    climb(2)

    for tree in range(2):
        stages[tree][2].receive_terms(highest.at[tree])
    highest_store.start()
    for tree in range(2):
        for k in range(1, spreads[tree][1]):
            spread_copy(tree, k, lax.rem(spreads[tree][2] + spreads[tree][1] - k, spreads[tree][1])).wait_recv()
    for tree in range(2):
        for n in range(3):
            stages[tree][n].finish()
    for tree in range(2):
        for k in range(1, 8):
            line_copy(tree, k, line_places[tree]).wait_send()
        for copy in spread_copies[tree]:
            copy.wait_send()
    for store in (leaf_store, highest_store, *keep_copies):
        store.wait()


def finish(
    leaf_hbm,
    highest_hbm,
    row_table_hbm,
    col_table_hbm,
    root_rows_hbm,
    root_cols_hbm,
    root_blocks_hbm,
    leaf_end,
    root_end,
    row_end,
    col_end,
    leaf_pass,
    highest,
    row_table,
    col_table,
    root_rows,
    root_cols,
    root_blocks,
    root_out,
    row_out,
    col_out,
    loads,
    stores,
    grams,
    batch,
    factors,
    root_left,
    root_right,
    block_stage,
):
    copies = [
        pltpu.make_async_copy(source, target, loads.at[n])
        for n, (source, target) in enumerate(
            [
                (highest_hbm, highest),
                (leaf_hbm, leaf_pass),
                (row_table_hbm, row_table),
                (col_table_hbm, col_table),
                (root_rows_hbm, root_rows),
                (root_cols_hbm, root_cols),
                (root_blocks_hbm, root_blocks),
            ]
        )
    ]
    for copy in copies:
        copy.start()
    results = [
        pltpu.make_async_copy(source, target, stores.at[n])
        for n, (source, target) in enumerate(
            [(leaf_pass, leaf_end), (row_out, row_end), (col_out, col_end), (root_out, root_end)]
        )
    ]
    copies[0].wait()
    copies[2].wait()
    copies[3].wait()
    for tree in range(2):
        grams[N_COL + N_ROW + tree, :, :RANK] = unpack(highest[tree])

    def spread_out(n, carry):
        for line in range(4):
            grams[line * 8 + n, :, :RANK] = unpack(row_table[line, n])
        for line in range(2):
            grams[N_COL + line * 8 + n, :, :RANK] = unpack(col_table[line, n])
        return carry

    lax.fori_loop(0, 8, spread_out, 0, unroll=8)
    to_lanes(grams, batch, ROOT_BATCH)
    factor(batch)
    copies[1].wait()
    results[0].start()
    from_lanes(batch, factors, (N_COL, N_ROW + 8))
    for tree, out in enumerate((row_out, col_out)):
        base = (N_COL + N_ROW + tree) * RANK
        even, odd = (factors[pl.ds(base + half, 32, stride=2), :][:, :RANK] for half in range(2))
        out[...] = jnp.concatenate([even, odd], 1)
    results[1].start()
    results[2].start()
    for copy in copies[4:]:
        copy.wait()

    def convert(first, entries, count, entry):
        def step(n, carry):
            entries[n] = entry(factors[pl.ds(pl.multiple_of((first + n) * RANK, RANK), RANK), :][:, :RANK])
            return carry

        lax.fori_loop(0, count, step, 0, unroll=16)

    convert(0, root_left, N_COL, table_entry)
    convert(N_COL, root_right, N_ROW, right_entry)
    couple(
        ROOT_PAIRS,
        root_blocks,
        block_stage,
        root_left,
        root_right,
        lambda pair: lax.rem(root_rows[0, 0, pair], N_X) * 8 + lax.div(root_rows[0, 0, pair], N_X),
        lambda pair: lax.rem(root_cols[0, 0, pair], N_CORE) * 8 + lax.div(root_cols[0, 0, pair], N_CORE),
        root_out,
    )
    results[3].start()
    for result in results:
        result.wait()


def tiled(array, rows):
    return array.reshape(rows // 8, 8, 32, 128).transpose(0, 2, 1, 3).reshape(rows * 32, 128)


def untiled(array, rows):
    return array.reshape(rows // 8, 32, 8, 128).transpose(0, 2, 1, 3).reshape(1, rows, RANK * RANK)


def body(
    row_bases,
    col_bases,
    row_transfer,
    col_transfer,
    row_order,
    col_order,
    leaf_pattern,
    leaf_blocks,
    root_rows,
    root_cols,
    root_blocks,
):
    vmem, smem = pltpu.VMEM, pltpu.SMEM
    dma = pltpu.SemaphoreType.DMA
    hbm = pl.BlockSpec(memory_space=pltpu.HBM)
    shape = jax.ShapeDtypeStruct
    packed = (32, 128)
    scratch = [
        vmem((LEAF_PAIRS * 32, 128), F32),
        dma((4,)),
        smem((1, 1, LEAF_DEV), jnp.int32),
        smem((1, 1, LEAF_DEV), jnp.int32),
        smem((1, 2, LEAF_PAIRS), jnp.int32),
        vmem((2, 512, 128), F32),
        vmem((2, 1024, 128), F32),
        vmem((2048, 128), BF16),
        dma((8,)),
        vmem((2 * 32, RANK, 128), F32),
        vmem((2 * LEAF_DEV, RANK, 128), F32),
        vmem((2 * 16, RANK, 128), F32),
        vmem((RANK, RANK, 128), F32),
        vmem((2 * LEAF_DEV * RANK, 128), F32),
        vmem((LEAF_DEV, 2 * RANK, RANK), BF16),
        vmem((LEAF_DEV, RANK, 2 * RANK), BF16),
        vmem((256, 128), F32),
        vmem((2, *packed), F32),
        vmem((2, *packed), F32),
        vmem((2, RANK, RANK), F32),
        vmem((2, *packed), F32),
        vmem((2, 8, *packed), F32),
        dma((2, 8)),
        dma((2, 8)),
        dma((2, N_X)),
        dma((2, N_X)),
    ]
    for tree in range(2):
        for depth in STAGES[tree]:
            size = 1 << depth
            scratch += [
                vmem((depth, *packed), F32),
                vmem((depth, RANK, RANK), F32),
                vmem((depth, *packed), F32),
                vmem((size, *packed), F32),
                dma((size,)),
                dma((depth,)),
                dma((size,)),
                dma((size,)),
            ]
    parts = pl.pallas_call(
        kernel,
        out_shape=(
            shape((LEAF_PAIRS * 32, 128), F32),
            shape((2, *packed), F32),
            shape((N_X, N_Y, *packed), F32),
            shape((N_CORE, N_Z, *packed), F32),
        ),
        in_specs=[hbm] * 8,
        out_specs=(hbm,) * 4,
        scratch_shapes=scratch,
        compiler_params=pltpu.CompilerParams(
            collective_id=0, has_side_effects=True, vmem_limit_bytes=62 * 2**20
        ),
    )(
        row_order,
        col_order,
        leaf_pattern,
        tiled(row_bases, LEAF_DEV),
        tiled(col_bases, LEAF_DEV),
        tiled(row_transfer, 2 * LEAF_DEV),
        tiled(col_transfer, 2 * LEAF_DEV),
        tiled(leaf_blocks, LEAF_PAIRS),
    )
    leaf_out, root_out, row_out, col_out = pl.pallas_call(
        finish,
        out_shape=(
            shape((LEAF_PAIRS * 32, 128), F32),
            shape((ROOT_PAIRS * 32, 128), F32),
            shape(packed, F32),
            shape(packed, F32),
        ),
        in_specs=[hbm] * 7,
        out_specs=(hbm,) * 4,
        scratch_shapes=[
            vmem((LEAF_PAIRS * 32, 128), F32),
            vmem((2, *packed), F32),
            vmem((N_X, N_Y, *packed), F32),
            vmem((N_CORE, N_Z, *packed), F32),
            smem((1, 1, ROOT_PAIRS), jnp.int32),
            smem((1, 1, ROOT_PAIRS), jnp.int32),
            vmem((1024, 128), BF16),
            vmem((ROOT_PAIRS * 32, 128), F32),
            vmem(packed, F32),
            vmem(packed, F32),
            dma((7,)),
            dma((4,)),
            vmem((ROOT_BATCH, RANK, 128), F32),
            vmem((RANK, RANK, 128), F32),
            vmem((ROOT_BATCH * RANK, 128), F32),
            vmem((N_COL, 2 * RANK, RANK), BF16),
            vmem((N_ROW, RANK, 2 * RANK), BF16),
            vmem((256, 128), F32),
        ],
        compiler_params=pltpu.CompilerParams(vmem_limit_bytes=62 * 2**20),
    )(*parts, root_rows, root_cols, tiled(root_blocks, ROOT_PAIRS))
    return (
        untiled(leaf_out, LEAF_PAIRS),
        untiled(root_out, ROOT_PAIRS),
        row_out.reshape(1, 1, RANK * RANK),
        col_out.reshape(1, 1, RANK * RANK),
    )


def solution(mesh):
    return jax.shard_map(
        body,
        mesh=mesh,
        in_specs=(
            P("row", "col", None),
            P("col", "row", None),
            P("row", "col", None),
            P("col", "row", None),
            P("row", "col", None),
            P("col", "row", None),
            P("row", "col", None),
            P("row", "col", None),
            P("row", "col", None),
            P("row", "col", None),
            P("row", "col", None),
        ),
        out_specs=(
            P("row", "col", None),
            P("row", "col", None),
            P("row", "col", None),
            P("col", "row", None),
        ),
        check_vma=False,
    )
```
